128 devices in a mesh: row: 32 (over z, x, core), col: 4 (over y).
Axes of the slice: x: 4, y: 4, z: 4, core: 2. Of those that a mesh axis runs over, the one named last changes fastest.
Arguments:
- gradients: bfloat16 [3, 512, 73728], P(None, 'row', 'col'), may hold values from -300 to 300
- parameter: float32 [512, 73728], P('row', 'col'), may hold values from -120 to 120
- row_state: float32 [512], P('row'), may hold values from 0.02 to 4.5, as said below
- col_state: float32 [73728], P('col'), may hold values from 0.02 to 4.5, as said below
Outputs:
- new_parameter: float32 [512, 73728], P('row', 'col')
- new_row_state: float32 [512], P('row')
- new_col_state: float32 [73728], P('col')
The draws below stay inside these ranges and needn't reach their ends.
Inputs may be any that keep to these rules, and one draw needn't show every extreme that they name: `row_state`: positive row moments. `col_state`: positive column moments.
All inputs are finite; a program needn't handle non-finite values.
Results may differ from the reference program's by a relative error of at most 0.0003.
Values sent between devices are 32-bit elements; how exact they have to be, the bound alone decides.
A program may use at most 64 MiB of HBM per device.

```python
import math
import jax
import jax.numpy as jnp
from jax import lax

COLS = 73728
ROW_DEV = 16
STEPS = 3
START = 100
ROWS = 512


def profile(key, length, spread_log, rise_log):
    rough = jax.random.uniform(key, (length,), jnp.float32, 0.0, spread_log)
    rising = jnp.arange(length, dtype=jnp.float32) / max(length - 1, 1) * rise_log
    return jnp.exp(0.5 * (rough + rising))


def block_levels(key):
    keys = jax.random.split(jax.random.fold_in(key, 5), 2)
    row_level = jax.random.uniform(keys[0], (ROWS // ROW_DEV,), jnp.float32, -1.0, 1.0)
    col_level = jax.random.uniform(keys[1], (8,), jnp.float32, -1.0, 1.0)
    return (jnp.repeat(row_level, ROW_DEV), jnp.repeat(col_level, COLS // 8))


def draw_gradients(key, part):
    row_level, col_level = block_levels(key)
    key = jax.random.fold_in(key, 11)
    keys = jax.random.split(key, 3)
    tile_gain = jnp.exp(row_level[:, None] * col_level[None, :])
    row_scale = profile(keys[0], ROWS, math.log(10.0), math.log(3.0))
    col_scale = profile(keys[1], COLS, math.log(10.0), 0.0)
    values = jnp.clip(jax.random.normal(keys[2], (STEPS, ROWS, COLS), jnp.float32), -4.0, 4.0)
    gain = tile_gain * row_scale[:, None] * col_scale[None, :]
    return (values * gain[None, :, :]).astype(jnp.bfloat16)


def draw_parameter(key, part):
    key = jax.random.fold_in(key, 23)
    keys = jax.random.split(key, 3)
    row_scale = profile(keys[0], ROWS, math.log(10.0), math.log(3.0))
    col_scale = profile(keys[1], COLS, math.log(10.0), 0.0)
    values = jnp.clip(jax.random.normal(keys[2], (ROWS, COLS), jnp.float32), -6.0, 6.0)
    return values * row_scale[:, None] * col_scale[None, :]


def draw_row_state(key, part):
    row_level, col_level = block_levels(key)
    key = jax.random.fold_in(key, 31)
    spread = jax.random.uniform(key, (ROWS,), jnp.float32, math.log(0.1), 0.0)
    return jnp.exp(spread + 1.5 * row_level)


def draw_col_state(key, part):
    row_level, col_level = block_levels(key)
    key = jax.random.fold_in(key, 37)
    spread = jax.random.uniform(key, (COLS,), jnp.float32, math.log(0.1), 0.0)
    return jnp.exp(spread + 1.5 * col_level)


def setup_inputs(seed: int = 0) -> dict:
    splits = jax.random.split(jax.random.key(seed), 5)
    return {
        "gradients": draw_gradients(jax.random.fold_in(splits[4], 71), 0),
        "parameter": draw_parameter(jax.random.fold_in(splits[4], 71), 0),
        "row_state": draw_row_state(jax.random.fold_in(splits[4], 71), 0),
        "col_state": draw_col_state(jax.random.fold_in(splits[4], 71), 0),
    }


def reference(gradients, parameter, row_state, col_state):
    elements = ROWS * COLS
    for index in range(STEPS):
        step_time = jnp.float32(START + 1 + index)
        forget = 1.0 - jnp.power(step_time, -0.8)
        step_rate = jnp.power(step_time, -0.5)
        current = gradients[index].astype(jnp.float32)
        squares = current * current
        row_state = forget * row_state + (1.0 - forget) * (lax.optimization_barrier(jnp.sum(squares, axis=1)) / COLS)
        col_state = forget * col_state + (1.0 - forget) * (lax.optimization_barrier(jnp.sum(squares, axis=0)) / ROWS)
        second = row_state[:, None] * col_state[None, :]
        update = current / jnp.sqrt(second)
        clip_factor = jnp.maximum(1.0, jnp.sqrt(jnp.sum(update * update) / elements))
        scale_now = jnp.sqrt(jnp.sum(parameter * parameter) / elements)
        parameter = parameter - step_rate * scale_now / clip_factor * update
    return (parameter, row_state, col_state)
```

```python
import functools

import jax
import jax.numpy as jnp
import numpy as np
from jax import lax
from jax.experimental import pallas as pl
from jax.experimental.pallas import tpu as pltpu
from jax.sharding import PartitionSpec as P

MESH = pl.DeviceIdType.MESH
START = 100
F32 = jnp.float32

NZ, NX, NK, NY = 4, 4, 2, 4
NROW, NALL = NZ * NX * NK, NZ * NX * NK * NY
STEPS, LROWS, LCOLS = 3, 16, 18432
ROWS, COLS = LROWS * NROW, LCOLS * NY
TILES = LCOLS // 128
HALF = TILES // 2
GROUPS = TILES // 8
CUT = 40
OUT_PARTS = 6


def far_first():
    dist = (0, 1, 2, 1)
    offs = [(dz, dx, dy, dk) for dz in range(NZ) for dx in range(NX) for dy in range(NY) for dk in range(NK)]
    offs = [o for o in offs if o != (0, 0, 0, 0)]
    return sorted(offs, key=lambda o: (-(dist[o[0]] + dist[o[1]] + dist[o[2]]), -o[3]))


def rates():
    out = []
    for k in range(STEPS):
        t = np.float32(START + 1 + k)
        forget = np.float32(1.0) - np.power(t, np.float32(-0.8))
        out.append((float(forget), float(np.float32(1.0) - forget), float(np.power(t, np.float32(-0.5)))))
    return out


def up(x, n):
    return pltpu.roll(x, 8 - n, 0)


def down(x, n):
    return pltpu.roll(x, n, 0)


def fold8(v):
    s = lax.broadcasted_iota(jnp.int32, (8, 128), 0)
    m4, m2, m1 = s < 4, lax.rem(s, 4) < 2, lax.rem(s, 2) < 1
    w = [jnp.where(m4, v[i], v[i + 4]) + up(jnp.where(m4, v[i + 4], v[i]), 4) for i in range(4)]
    x = [jnp.where(m2, w[i] + up(w[i], 2), w[i + 2] + down(w[i + 2], 2)) for i in range(2)]
    return jnp.where(m1, x[0] + up(x[0], 1), x[1] + down(x[1], 1))


def kernel(
    grad_hbm, param_hbm, row_ref, col_ref,
    out_hbm, newrow_ref, newcol_ref,
    g, p, o, u, s, pin, xa, za, zb, xb, rowbox, w, win, wsum, c, rc, bbox,
    load_sem, out_sem, pair_s, pair_r, xa_s, xa_r, za_s, za_r, zb_s, zb_r, xb_s, xb_r,
    row_s, row_r, w_s, w_r, c_s, c_r, b_s, b_r, sem_b, sem_c, sem_d,
):
    rate = rates()
    row, y = lax.axis_index("row"), lax.axis_index("col")
    z, x, k = lax.div(row, 8), lax.rem(lax.div(row, 2), 4), lax.rem(row, 2)

    def at(dz=0, dx=0, dy=0, dk=0):
        zz = lax.rem(z + dz, NZ) if dz else z
        xx = lax.rem(x + dx, NX) if dx else x
        kk = 1 - k if dk else k
        yy = lax.rem(y + dy, NY) if dy else y
        return (zz * 8 + xx * 2 + kk, yy)

    pair = at(dk=1)
    xs = [at(dx=d) for d in (2, 1, 3)]
    zs = [at(dz=d) for d in (2, 1, 3)]
    ys = [at(dy=d) for d in (2, 1, 3)]

    def signal(sem, devices):
        for d in devices:
            pl.semaphore_signal(sem, inc=1, device_id=d, device_id_type=MESH)

    def remote(src, dst, send, recv, device):
        return pltpu.make_async_remote_copy(src, dst, send, recv, device_id=device, device_id_type=MESH)

    loads = [pltpu.make_async_copy(grad_hbm.at[i], g.at[i], load_sem.at[i]) for i in range(STEPS)]
    loads.append(pltpu.make_async_copy(param_hbm, p, load_sem.at[STEPS]))
    for load in loads:
        load.start()
    barrier = pltpu.get_barrier_semaphore()
    signal(barrier, [*zs, *xs, *ys, pair])

    mine = pl.multiple_of(k * HALF, 8)
    other = pl.multiple_of((1 - k) * HALF, 8)
    lane = lax.broadcasted_iota(jnp.int32, (LROWS, 128), 1)

    def tile(ref, i, n, j):
        return ref[i, :, pl.ds(pl.multiple_of(n * 1024 + j * 128, 128), 128)].astype(F32)

    def squares(i, packed):
        def group(n, rows):
            sums = []
            for j in range(8):
                a = tile(g, i, n, j)
                a = a * a
                rows = rows + a
                sums.append(a[:8] + a[8:])
            s[i, pl.ds(pl.multiple_of(n * 8, 8), 8), :] = fold8(sums)
            return rows

        rows = lax.fori_loop(0, GROUPS, group, jnp.zeros((LROWS, 128), F32))
        return jnp.where(lane == i, jnp.sum(rows, axis=1, keepdims=True), packed)

    def pair_copy(i):
        return remote(s.at[i, pl.ds(other, HALF)], pin.at[i], pair_s.at[i], pair_r.at[i], pair)

    def first_round(i):
        pair_copy(i).wait_recv()
        xa[i, x] = s[i, pl.ds(mine, CUT), :] + pin[i, :CUT]
        za[i, z] = s[i, pl.ds(mine + CUT, HALF - CUT), :] + pin[i, CUT:]
        for a, b in zip(xs, zs):
            remote(xa.at[i, x], xa.at[i, x], xa_s.at[i], xa_r.at[i], a).start()
            remote(za.at[i, z], za.at[i, z], za_s.at[i], za_r.at[i], b).start()

    def three(ref, send, recv):
        return remote(ref.at[pl.ds(0, 3)], ref.at[pl.ds(0, 3)], send, recv, pair)

    def four(ref, i):
        return (ref[i, 0] + ref[i, 1]) + (ref[i, 2] + ref[i, 3])

    def second_round(i):
        three(xa.at[i], xa_s.at[i], xa_r.at[i]).wait_recv()
        zb[i, z] = four(xa, i)
        for b in zs:
            remote(zb.at[i, z], zb.at[i, z], zb_s.at[i], zb_r.at[i], b).start()
        three(za.at[i], za_s.at[i], za_r.at[i]).wait_recv()
        xb[i, x] = four(za, i)
        for a in xs:
            remote(xb.at[i, x], xb.at[i, x], xb_s.at[i], xb_r.at[i], a).start()

    packed = jnp.zeros((LROWS, 128), F32)
    loads[0].wait()
    packed = squares(0, packed)
    pl.semaphore_wait(barrier, 10)
    pair_copy(0).start()
    signal(sem_b, [pair])
    loads[1].wait()
    packed = squares(1, packed)
    pair_copy(1).start()
    pl.semaphore_wait(sem_b, 1)
    signal(sem_c, xs)
    first_round(0)
    loads[2].wait()
    packed = squares(2, packed)
    pair_copy(2).start()
    rowbox[y] = packed
    for d in ys:
        remote(rowbox.at[y], rowbox.at[y], row_s, row_r, d).start()
    first_round(1)
    first_round(2)
    pl.semaphore_wait(sem_c, 3)
    signal(sem_d, zs)

    loads[STEPS].wait()

    def norm(n, acc):
        for j in range(8):
            a = p[:, pl.ds(pl.multiple_of(n * 1024 + j * 128, 128), 128)]
            a = a * a
            acc = acc + (a[:8] + a[8:])
        return acc

    psum = lax.fori_loop(0, GROUPS, norm, jnp.zeros((8, 128), F32))

    for i in range(STEPS):
        second_round(i)

    three(rowbox, row_s, row_r).wait_recv()
    total = (rowbox[0] + rowbox[1]) + (rowbox[2] + rowbox[3])
    i0 = lax.broadcasted_iota(jnp.int32, (LROWS, LROWS), 0)
    i1 = lax.broadcasted_iota(jnp.int32, (LROWS, LROWS), 1)
    state = jnp.sum(jnp.where(i0 == i1, row_ref[...], 0.0), axis=1, keepdims=True)
    rr = []
    for i in range(STEPS):
        state = rate[i][0] * state + rate[i][1] * (total[:, i : i + 1] / COLS)
        rr.append(jnp.broadcast_to(lax.rsqrt(state), (LROWS, 128)))
    newrow_ref[...] = jnp.sum(jnp.where(i0 == i1, state, 0.0), axis=0, keepdims=True)

    def products(n, _):
        sums = [[] for _ in range(6)]
        for j in range(8):
            a = [tile(g, i, n, j) * rr[i] for i in range(STEPS)]
            q = p[:, pl.ds(pl.multiple_of(n * 1024 + j * 128, 128), 128)]
            for m, v in enumerate((a[0] * a[0], a[1] * a[1], a[2] * a[2], a[0] * a[1], a[0] * q, a[1] * q)):
                sums[m].append(v[:8] + v[8:])
        for m in range(6):
            w[m, pl.ds(pl.multiple_of(n * 8, 8), 8), :] = fold8(sums[m])
        return 0

    lax.fori_loop(0, GROUPS, products, 0)
    w_copy = remote(w.at[:, pl.ds(other, HALF)], win, w_s, w_r, pair)
    w_copy.start()
    w_copy.wait_recv()
    for m in range(6):
        wsum[m] = w[m, pl.ds(mine, HALF), :] + win[m]

    colstate = [col_ref[pl.ds(mine, CUT), :], col_ref[pl.ds(mine + CUT, HALF - CUT), :]]

    def c_copy(i):
        return remote(c.at[i, pl.ds(mine, HALF)], c.at[i, pl.ds(mine, HALF)], c_s.at[i], c_r.at[i], pair)

    for i in range(STEPS):
        three(zb.at[i], zb_s.at[i], zb_r.at[i]).wait_recv()
        three(xb.at[i], xb_s.at[i], xb_r.at[i]).wait_recv()
        for part, ref, start, size in ((0, zb, 0, CUT), (1, xb, CUT, HALF - CUT)):
            colstate[part] = rate[i][0] * colstate[part] + rate[i][1] * (four(ref, i) / ROWS)
            c[i, pl.ds(mine + start, size), :] = colstate[part]
            rc[i, pl.ds(mine + start, size), :] = lax.rsqrt(colstate[part])
        c_copy(i).start()
    acc = [jnp.zeros((8, 128), F32) for _ in range(6)]
    for n in range(HALF // 8):
        q = [rc[i, pl.ds(pl.multiple_of(mine + n * 8, 8), 8), :] for i in range(STEPS)]
        f = (q[0] * q[0], q[1] * q[1], q[2] * q[2], q[0] * q[1], q[0], q[1])
        acc = [acc[m] + f[m] * wsum[m, n * 8 : n * 8 + 8, :] for m in range(6)]
    sums = jnp.sum(fold8([*acc, psum, jnp.zeros((8, 128), F32)]), axis=1, keepdims=True)
    j0 = lax.broadcasted_iota(jnp.int32, (8, 128), 0)
    j1 = lax.broadcasted_iota(jnp.int32, (8, 128), 1)
    me = y * NROW + row
    bbox[me] = jnp.sum(jnp.where(j0 == j1, sums, 0.0), axis=0, keepdims=True)
    pl.semaphore_wait(sem_d, 3)
    for off in far_first():
        remote(bbox.at[me], bbox.at[me], b_s, b_r, at(*off)).start()

    for i in range(STEPS):
        remote(c.at[i, pl.ds(other, HALF)], c.at[i, pl.ds(other, HALF)], c_s.at[i], c_r.at[i], pair).wait_recv()
        rc[i, pl.ds(other, HALF), :] = lax.rsqrt(c[i, pl.ds(other, HALF), :])
    newcol_ref[...] = c[STEPS - 1]

    def updates(n, _):
        for i in range(STEPS):
            q = rc[i, pl.ds(pl.multiple_of(n * 8, 8), 8), :]
            for j in range(8):
                u[i, :, pl.ds(pl.multiple_of(n * 1024 + j * 128, 128), 128)] = tile(g, i, n, j) * rr[i] * q[j : j + 1]
        return 0

    lax.fori_loop(0, GROUPS, updates, 0)

    b_all = bbox.at[pl.ds(0, NALL - 1)]
    remote(b_all, b_all, b_s, b_r, pair).wait_recv()
    sums = jnp.sum(bbox[...], axis=0)
    j1 = lax.broadcasted_iota(jnp.int32, (1, 128), 1)
    uu0, uu1, uu2, u01, pu0, pu1, pp = [
        jnp.sum(jnp.where(j1 == m, sums, 0.0), axis=1, keepdims=True) for m in range(7)
    ]
    count = float(ROWS * COLS)
    clip = [jnp.maximum(1.0, jnp.sqrt(v / count)) for v in (uu0, uu1, uu2)]
    f0 = rate[0][2] * jnp.sqrt(pp / count) / clip[0]
    pp = pp - 2.0 * f0 * pu0 + f0 * f0 * uu0
    f1 = rate[1][2] * jnp.sqrt(pp / count) / clip[1]
    pp = pp - 2.0 * f1 * (pu1 - f0 * u01) + f1 * f1 * uu1
    f2 = rate[2][2] * jnp.sqrt(pp / count) / clip[2]
    f = [jnp.broadcast_to(v, (LROWS, 128)) for v in (f0, f1, f2)]

    width = LCOLS // OUT_PARTS
    outs = []
    for part in range(OUT_PARTS):

        def final(n, _, part=part):
            for j in range(8):
                cols = pl.ds(pl.multiple_of(part * width + n * 1024 + j * 128, 128), 128)
                o[:, cols] = p[:, cols] - f[0] * u[0, :, cols] - f[1] * u[1, :, cols] - f[2] * u[2, :, cols]
            return 0

        lax.fori_loop(0, width // 1024, final, 0)
        cols = pl.ds(part * width, width)
        outs.append(pltpu.make_async_copy(o.at[:, cols], out_hbm.at[:, cols], out_sem.at[part]))
        outs[-1].start()

    for i in range(STEPS):
        pair_copy(i).wait_send()
        three(xa.at[i], xa_s.at[i], xa_r.at[i]).wait_send()
        three(za.at[i], za_s.at[i], za_r.at[i]).wait_send()
        three(zb.at[i], zb_s.at[i], zb_r.at[i]).wait_send()
        three(xb.at[i], xb_s.at[i], xb_r.at[i]).wait_send()
        c_copy(i).wait_send()
    three(rowbox, row_s, row_r).wait_send()
    w_copy.wait_send()
    remote(b_all, b_all, b_s, b_r, pair).wait_send()
    for out in outs:
        out.wait()


def local(gradients, parameter, row_state, col_state):
    vmem = pl.BlockSpec(memory_space=pltpu.VMEM)
    hbm = pl.BlockSpec(memory_space=pl.ANY)
    dma = pltpu.SemaphoreType.DMA
    three = dma((STEPS,))
    new_param, new_row, new_col = pl.pallas_call(
        kernel,
        name="adafactor",
        out_shape=(
            jax.ShapeDtypeStruct((LROWS, LCOLS), F32),
            jax.ShapeDtypeStruct((1, LROWS), F32),
            jax.ShapeDtypeStruct((TILES, 128), F32),
        ),
        in_specs=[hbm, hbm, vmem, vmem],
        out_specs=(hbm, vmem, vmem),
        scratch_shapes=[
            pltpu.VMEM((STEPS, LROWS, LCOLS), jnp.bfloat16),
            pltpu.VMEM((LROWS, LCOLS), F32),
            pltpu.VMEM((LROWS, LCOLS), F32),
            pltpu.VMEM((STEPS, LROWS, LCOLS), F32),
            pltpu.VMEM((STEPS, TILES, 128), F32),
            pltpu.VMEM((STEPS, HALF, 128), F32),
            pltpu.VMEM((STEPS, NX, CUT, 128), F32),
            pltpu.VMEM((STEPS, NZ, HALF - CUT, 128), F32),
            pltpu.VMEM((STEPS, NZ, CUT, 128), F32),
            pltpu.VMEM((STEPS, NX, HALF - CUT, 128), F32),
            pltpu.VMEM((NY, LROWS, 128), F32),
            pltpu.VMEM((6, TILES, 128), F32),
            pltpu.VMEM((6, HALF, 128), F32),
            pltpu.VMEM((6, HALF, 128), F32),
            pltpu.VMEM((STEPS, TILES, 128), F32),
            pltpu.VMEM((STEPS, TILES, 128), F32),
            pltpu.VMEM((NALL, 1, 128), F32),
            dma((STEPS + 1,)), dma((OUT_PARTS,)),
            three, three, three, three, three, three, three, three, three, three,
            dma, dma, dma, dma, three, three, dma, dma,
            pltpu.SemaphoreType.REGULAR, pltpu.SemaphoreType.REGULAR, pltpu.SemaphoreType.REGULAR,
        ],
        compiler_params=pltpu.CompilerParams(
            collective_id=0, has_side_effects=True, vmem_limit_bytes=40 * 2**20
        ),
        cost_estimate=pl.CostEstimate(flops=20_000_000, bytes_accessed=4_200_000, transcendentals=100_000),
    )(gradients, parameter, row_state.reshape(1, LROWS), col_state.reshape(TILES, 128))
    return new_param, new_row.reshape(LROWS), new_col.reshape(LCOLS)


def solution(mesh):
    placed = (P(None, "row", "col"), P("row", "col"), P("row"), P("col"))
    return jax.shard_map(
        local,
        mesh=mesh,
        in_specs=placed,
        out_specs=(P("row", "col"), P("row"), P("col")),
        check_vma=False,
    )
```

```python
import functools

import jax
import jax.numpy as jnp
import numpy as np
from jax import lax
from jax.experimental import pallas as pl
from jax.experimental.pallas import tpu as pltpu
from jax.sharding import PartitionSpec as P

MESH = pl.DeviceIdType.MESH
START = 100
F32 = jnp.float32

NZ, NX, NK, NY = 4, 4, 2, 4
NROW, NALL = NZ * NX * NK, NZ * NX * NK * NY
STEPS, LROWS, LCOLS = 3, 16, 18432
ROWS, COLS = LROWS * NROW, LCOLS * NY
TILES = LCOLS // 128
HALF = TILES // 2
GROUPS = TILES // 8
CUT = 40
OUT_PARTS = 6


def far_first():
    dist = (0, 1, 2, 1)
    offs = [(dz, dx, dy, dk) for dz in range(NZ) for dx in range(NX) for dy in range(NY) for dk in range(NK)]
    offs = [o for o in offs if o != (0, 0, 0, 0)]
    return sorted(offs, key=lambda o: (-(dist[o[0]] + dist[o[1]] + dist[o[2]]), -o[3]))


def rates():
    out = []
    for k in range(STEPS):
        t = np.float32(START + 1 + k)
        forget = np.float32(1.0) - np.power(t, np.float32(-0.8))
        out.append((float(forget), float(np.float32(1.0) - forget), float(np.power(t, np.float32(-0.5)))))
    return out


def up(x, n):
    return pltpu.roll(x, 8 - n, 0)


def down(x, n):
    return pltpu.roll(x, n, 0)


def fold8(v):
    s = lax.broadcasted_iota(jnp.int32, (8, 128), 0)
    m4, m2, m1 = s < 4, lax.rem(s, 4) < 2, lax.rem(s, 2) < 1
    w = [jnp.where(m4, v[i], v[i + 4]) + up(jnp.where(m4, v[i + 4], v[i]), 4) for i in range(4)]
    x = [jnp.where(m2, w[i] + up(w[i], 2), w[i + 2] + down(w[i + 2], 2)) for i in range(2)]
    return jnp.where(m1, x[0] + up(x[0], 1), x[1] + down(x[1], 1))


def kernel(
    grad_hbm, param_hbm, row_hbm, col_hbm,
    p, u, factor_ref, newrow_ref, newcol_ref,
    g, row_ref, col_ref, s, pin, xa, za, zb, xb, rowbox, w, win, wsum, c, rc, bbox,
    load_sem, pair_s, pair_r, xa_s, xa_r, za_s, za_r, zb_s, zb_r, xb_s, xb_r,
    row_s, row_r, w_s, w_r, c_s, c_r, b_s, b_r, sem_b, sem_c, sem_d,
):
    rate = rates()
    row, y = lax.axis_index("row"), lax.axis_index("col")
    z, x, k = lax.div(row, 8), lax.rem(lax.div(row, 2), 4), lax.rem(row, 2)

    def at(dz=0, dx=0, dy=0, dk=0):
        zz = lax.rem(z + dz, NZ) if dz else z
        xx = lax.rem(x + dx, NX) if dx else x
        kk = 1 - k if dk else k
        yy = lax.rem(y + dy, NY) if dy else y
        return (zz * 8 + xx * 2 + kk, yy)

    pair = at(dk=1)
    xs = [at(dx=d) for d in (2, 1, 3)]
    zs = [at(dz=d) for d in (2, 1, 3)]
    ys = [at(dy=d) for d in (2, 1, 3)]

    def signal(sem, devices):
        for d in devices:
            pl.semaphore_signal(sem, inc=1, device_id=d, device_id_type=MESH)

    def remote(src, dst, send, recv, device):
        return pltpu.make_async_remote_copy(src, dst, send, recv, device_id=device, device_id_type=MESH)

    loads = [pltpu.make_async_copy(grad_hbm.at[i], g.at[i], load_sem.at[i]) for i in range(STEPS)]
    loads.append(pltpu.make_async_copy(param_hbm, p, load_sem.at[STEPS]))
    loads.append(pltpu.make_async_copy(col_hbm, col_ref, load_sem.at[STEPS + 1]))
    loads.append(pltpu.make_async_copy(row_hbm, row_ref, load_sem.at[STEPS + 2]))
    for load in loads:
        load.start()
    barrier = pltpu.get_barrier_semaphore()
    signal(barrier, [*zs, *xs, *ys, pair])

    mine = pl.multiple_of(k * HALF, 8)
    other = pl.multiple_of((1 - k) * HALF, 8)
    lane = lax.broadcasted_iota(jnp.int32, (LROWS, 128), 1)

    def tile(ref, i, n, j):
        return ref[i, :, pl.ds(pl.multiple_of(n * 1024 + j * 128, 128), 128)].astype(F32)

    def squares(i, packed):
        def group(n, rows):
            sums = []
            for j in range(8):
                a = tile(g, i, n, j)
                a = a * a
                rows = rows + a
                sums.append(a[:8] + a[8:])
            s[i, pl.ds(pl.multiple_of(n * 8, 8), 8), :] = fold8(sums)
            return rows

        rows = lax.fori_loop(0, GROUPS, group, jnp.zeros((LROWS, 128), F32))
        return jnp.where(lane == i, jnp.sum(rows, axis=1, keepdims=True), packed)

    def pair_copy(i):
        return remote(s.at[i, pl.ds(other, HALF)], pin.at[i], pair_s.at[i], pair_r.at[i], pair)

    def first_round(i):
        pair_copy(i).wait_recv()
        xa[i, x] = s[i, pl.ds(mine, CUT), :] + pin[i, :CUT]
        za[i, z] = s[i, pl.ds(mine + CUT, HALF - CUT), :] + pin[i, CUT:]
        for a, b in zip(xs, zs):
            remote(xa.at[i, x], xa.at[i, x], xa_s.at[i], xa_r.at[i], a).start()
            remote(za.at[i, z], za.at[i, z], za_s.at[i], za_r.at[i], b).start()

    def three(ref, send, recv):
        return remote(ref.at[pl.ds(0, 3)], ref.at[pl.ds(0, 3)], send, recv, pair)

    def four(ref, i):
        return (ref[i, 0] + ref[i, 1]) + (ref[i, 2] + ref[i, 3])

    def second_round(i):
        three(xa.at[i], xa_s.at[i], xa_r.at[i]).wait_recv()
        zb[i, z] = four(xa, i)
        for b in zs:
            remote(zb.at[i, z], zb.at[i, z], zb_s.at[i], zb_r.at[i], b).start()
        three(za.at[i], za_s.at[i], za_r.at[i]).wait_recv()
        xb[i, x] = four(za, i)
        for a in xs:
            remote(xb.at[i, x], xb.at[i, x], xb_s.at[i], xb_r.at[i], a).start()

    packed = jnp.zeros((LROWS, 128), F32)
    loads[0].wait()
    packed = squares(0, packed)
    pl.semaphore_wait(barrier, 10)
    pair_copy(0).start()
    signal(sem_b, [pair])
    loads[1].wait()
    packed = squares(1, packed)
    pair_copy(1).start()
    pl.semaphore_wait(sem_b, 1)
    signal(sem_c, xs)
    first_round(0)
    loads[2].wait()
    packed = squares(2, packed)
    pair_copy(2).start()
    rowbox[y] = packed
    for d in ys:
        remote(rowbox.at[y], rowbox.at[y], row_s, row_r, d).start()
    first_round(1)
    first_round(2)
    pl.semaphore_wait(sem_c, 3)
    signal(sem_d, zs)

    loads[STEPS].wait()

    def norm(n, acc):
        for j in range(8):
            a = p[:, pl.ds(pl.multiple_of(n * 1024 + j * 128, 128), 128)]
            a = a * a
            acc = acc + (a[:8] + a[8:])
        return acc

    psum = lax.fori_loop(0, GROUPS, norm, jnp.zeros((8, 128), F32))

    for i in range(STEPS):
        second_round(i)

    three(rowbox, row_s, row_r).wait_recv()
    total = (rowbox[0] + rowbox[1]) + (rowbox[2] + rowbox[3])
    loads[STEPS + 2].wait()
    i0 = lax.broadcasted_iota(jnp.int32, (LROWS, LROWS), 0)
    i1 = lax.broadcasted_iota(jnp.int32, (LROWS, LROWS), 1)
    state = jnp.sum(jnp.where(i0 == i1, row_ref[...], 0.0), axis=1, keepdims=True)
    rr = []
    for i in range(STEPS):
        state = rate[i][0] * state + rate[i][1] * (total[:, i : i + 1] / COLS)
        rr.append(jnp.broadcast_to(lax.rsqrt(state), (LROWS, 128)))
    newrow_ref[...] = jnp.sum(jnp.where(i0 == i1, state, 0.0), axis=0, keepdims=True)

    def products(n, _):
        sums = [[] for _ in range(6)]
        for j in range(8):
            a = [tile(g, i, n, j) * rr[i] for i in range(STEPS)]
            q = p[:, pl.ds(pl.multiple_of(n * 1024 + j * 128, 128), 128)]
            for m, v in enumerate((a[0] * a[0], a[1] * a[1], a[2] * a[2], a[0] * a[1], a[0] * q, a[1] * q)):
                sums[m].append(v[:8] + v[8:])
        for m in range(6):
            w[m, pl.ds(pl.multiple_of(n * 8, 8), 8), :] = fold8(sums[m])
        return 0

    lax.fori_loop(0, GROUPS, products, 0)
    w_copy = remote(w.at[:, pl.ds(other, HALF)], win, w_s, w_r, pair)
    w_copy.start()
    w_copy.wait_recv()
    for m in range(6):
        wsum[m] = w[m, pl.ds(mine, HALF), :] + win[m]

    loads[STEPS + 1].wait()
    colstate = [col_ref[pl.ds(mine, CUT), :], col_ref[pl.ds(mine + CUT, HALF - CUT), :]]

    def c_copy(i):
        return remote(c.at[i, pl.ds(mine, HALF)], c.at[i, pl.ds(mine, HALF)], c_s.at[i], c_r.at[i], pair)

    for i in range(STEPS):
        three(zb.at[i], zb_s.at[i], zb_r.at[i]).wait_recv()
        three(xb.at[i], xb_s.at[i], xb_r.at[i]).wait_recv()
        for part, ref, start, size in ((0, zb, 0, CUT), (1, xb, CUT, HALF - CUT)):
            colstate[part] = rate[i][0] * colstate[part] + rate[i][1] * (four(ref, i) / ROWS)
            c[i, pl.ds(mine + start, size), :] = colstate[part]
            rc[i, pl.ds(mine + start, size), :] = lax.rsqrt(colstate[part])
        c_copy(i).start()
    acc = [jnp.zeros((8, 128), F32) for _ in range(6)]
    for n in range(HALF // 8):
        q = [rc[i, pl.ds(pl.multiple_of(mine + n * 8, 8), 8), :] for i in range(STEPS)]
        f = (q[0] * q[0], q[1] * q[1], q[2] * q[2], q[0] * q[1], q[0], q[1])
        acc = [acc[m] + f[m] * wsum[m, n * 8 : n * 8 + 8, :] for m in range(6)]
    sums = jnp.sum(fold8([*acc, psum, jnp.zeros((8, 128), F32)]), axis=1, keepdims=True)
    j0 = lax.broadcasted_iota(jnp.int32, (8, 128), 0)
    j1 = lax.broadcasted_iota(jnp.int32, (8, 128), 1)
    me = y * NROW + row
    bbox[me] = jnp.sum(jnp.where(j0 == j1, sums, 0.0), axis=0, keepdims=True)
    pl.semaphore_wait(sem_d, 3)
    for off in far_first():
        remote(bbox.at[me], bbox.at[me], b_s, b_r, at(*off)).start()

    for i in range(STEPS):
        remote(c.at[i, pl.ds(other, HALF)], c.at[i, pl.ds(other, HALF)], c_s.at[i], c_r.at[i], pair).wait_recv()
        rc[i, pl.ds(other, HALF), :] = lax.rsqrt(c[i, pl.ds(other, HALF), :])
    newcol_ref[...] = c[STEPS - 1]

    def updates(n, _):
        for i in range(STEPS):
            q = rc[i, pl.ds(pl.multiple_of(n * 8, 8), 8), :]
            for j in range(8):
                u[i, :, pl.ds(pl.multiple_of(n * 1024 + j * 128, 128), 128)] = tile(g, i, n, j) * rr[i] * q[j : j + 1]
        return 0

    lax.fori_loop(0, GROUPS, updates, 0)

    b_all = bbox.at[pl.ds(0, NALL - 1)]
    remote(b_all, b_all, b_s, b_r, pair).wait_recv()
    sums = jnp.sum(bbox[...], axis=0)
    j1 = lax.broadcasted_iota(jnp.int32, (1, 128), 1)
    uu0, uu1, uu2, u01, pu0, pu1, pp = [
        jnp.sum(jnp.where(j1 == m, sums, 0.0), axis=1, keepdims=True) for m in range(7)
    ]
    count = float(ROWS * COLS)
    clip = [jnp.maximum(1.0, jnp.sqrt(v / count)) for v in (uu0, uu1, uu2)]
    f0 = rate[0][2] * jnp.sqrt(pp / count) / clip[0]
    pp = pp - 2.0 * f0 * pu0 + f0 * f0 * uu0
    f1 = rate[1][2] * jnp.sqrt(pp / count) / clip[1]
    pp = pp - 2.0 * f1 * (pu1 - f0 * u01) + f1 * f1 * uu1
    f2 = rate[2][2] * jnp.sqrt(pp / count) / clip[2]
    for i, v in enumerate((f0, f1, f2)):
        factor_ref[i] = jnp.broadcast_to(v, (8, 128))

    for i in range(STEPS):
        pair_copy(i).wait_send()
        three(xa.at[i], xa_s.at[i], xa_r.at[i]).wait_send()
        three(za.at[i], za_s.at[i], za_r.at[i]).wait_send()
        three(zb.at[i], zb_s.at[i], zb_r.at[i]).wait_send()
        three(xb.at[i], xb_s.at[i], xb_r.at[i]).wait_send()
        c_copy(i).wait_send()
    three(rowbox, row_s, row_r).wait_send()
    w_copy.wait_send()
    remote(b_all, b_all, b_s, b_r, pair).wait_send()


def finish(p, u, factor_ref, newrow_ref, newcol_ref, out_hbm, row_hbm, col_hbm, o, out_sem, row_sem, col_sem):
    f = [jnp.concatenate([factor_ref[i], factor_ref[i]], axis=0) for i in range(STEPS)]
    width = LCOLS // OUT_PARTS
    outs = [
        pltpu.make_async_copy(newcol_ref, col_hbm, col_sem),
        pltpu.make_async_copy(newrow_ref, row_hbm, row_sem),
    ]
    for out in outs:
        out.start()
    for part in range(OUT_PARTS):

        def final(n, _, part=part):
            for j in range(8):
                cols = pl.ds(pl.multiple_of(part * width + n * 1024 + j * 128, 128), 128)
                o[:, cols] = p[:, cols] - f[0] * u[0, :, cols] - f[1] * u[1, :, cols] - f[2] * u[2, :, cols]
            return 0

        lax.fori_loop(0, width // 1024, final, 0)
        cols = pl.ds(part * width, width)
        outs.append(pltpu.make_async_copy(o.at[:, cols], out_hbm.at[:, cols], out_sem.at[part]))
        outs[-1].start()
    for out in outs:
        out.wait()


def local(gradients, parameter, row_state, col_state):
    vmem = pl.BlockSpec(memory_space=pltpu.VMEM)
    hbm = pl.BlockSpec(memory_space=pltpu.HBM)
    dma = pltpu.SemaphoreType.DMA
    three = dma((STEPS,))
    slab = jax.ShapeDtypeStruct((LROWS, LCOLS), F32)
    small = (jax.ShapeDtypeStruct((1, LROWS), F32), jax.ShapeDtypeStruct((TILES, 128), F32))
    state = pl.pallas_call(
        kernel,
        name="exchange",
        out_shape=(
            slab,
            jax.ShapeDtypeStruct((STEPS, LROWS, LCOLS), F32),
            jax.ShapeDtypeStruct((STEPS, 8, 128), F32),
            *small,
        ),
        in_specs=[hbm] * 4,
        out_specs=(vmem,) * 5,
        scratch_shapes=[
            pltpu.VMEM((STEPS, LROWS, LCOLS), jnp.bfloat16),
            pltpu.VMEM((1, LROWS), F32),
            pltpu.VMEM((TILES, 128), F32),
            pltpu.VMEM((STEPS, TILES, 128), F32),
            pltpu.VMEM((STEPS, HALF, 128), F32),
            pltpu.VMEM((STEPS, NX, CUT, 128), F32),
            pltpu.VMEM((STEPS, NZ, HALF - CUT, 128), F32),
            pltpu.VMEM((STEPS, NZ, CUT, 128), F32),
            pltpu.VMEM((STEPS, NX, HALF - CUT, 128), F32),
            pltpu.VMEM((NY, LROWS, 128), F32),
            pltpu.VMEM((6, TILES, 128), F32),
            pltpu.VMEM((6, HALF, 128), F32),
            pltpu.VMEM((6, HALF, 128), F32),
            pltpu.VMEM((STEPS, TILES, 128), F32),
            pltpu.VMEM((STEPS, TILES, 128), F32),
            pltpu.VMEM((NALL, 1, 128), F32),
            dma((STEPS + 3,)),
            three, three, three, three, three, three, three, three, three, three,
            dma, dma, dma, dma, three, three, dma, dma,
            pltpu.SemaphoreType.REGULAR, pltpu.SemaphoreType.REGULAR, pltpu.SemaphoreType.REGULAR,
        ],
        compiler_params=pltpu.CompilerParams(
            collective_id=0, has_side_effects=True, vmem_limit_bytes=40 * 2**20
        ),
        cost_estimate=pl.CostEstimate(flops=20_000_000, bytes_accessed=4_200_000, transcendentals=100_000),
    )(*[pltpu.with_memory_space_constraint(a, pltpu.HBM) for a in (gradients, parameter, row_state.reshape(1, LROWS), col_state.reshape(TILES, 128))])
    new_param, new_row, new_col = pl.pallas_call(
        finish,
        name="finish",
        out_shape=(slab, *small),
        in_specs=[vmem] * 5,
        out_specs=(hbm,) * 3,
        scratch_shapes=[pltpu.VMEM((LROWS, LCOLS), F32), dma((OUT_PARTS,)), dma, dma],
        compiler_params=pltpu.CompilerParams(vmem_limit_bytes=40 * 2**20),
        cost_estimate=pl.CostEstimate(flops=2_000_000, bytes_accessed=1_200_000, transcendentals=0),
    )(*state)
    return new_param, new_row.reshape(LROWS), new_col.reshape(LCOLS)


def solution(mesh):
    placed = (P(None, "row", "col"), P("row", "col"), P("row"), P("col"))
    return jax.shard_map(
        local,
        mesh=mesh,
        in_specs=placed,
        out_specs=(P("row", "col"), P("row"), P("col")),
        check_vma=False,
    )
```

```python
import functools

import jax
import jax.numpy as jnp
import numpy as np
from jax import lax
from jax.experimental import pallas as pl
from jax.experimental.pallas import tpu as pltpu
from jax.sharding import PartitionSpec as P

MESH = pl.DeviceIdType.MESH
START = 100
F32 = jnp.float32

NZ, NX, NK, NY = 4, 4, 2, 4
NROW, NALL = NZ * NX * NK, NZ * NX * NK * NY
STEPS, LROWS, LCOLS = 3, 16, 18432
ROWS, COLS = LROWS * NROW, LCOLS * NY
TILES = LCOLS // 128
HALF, HCOLS = TILES // 2, LCOLS // 2
PIECES = 8
PTILES = HALF // PIECES
PCOLS = PTILES * 128
SROWS = 32
WROWS = 56
PRODUCTS = 6
OUT_PARTS = 3


def far_first():
    dist = (0, 1, 2, 1)
    offs = [(dz, dx, dy, dk) for dz in range(NZ) for dx in range(NX) for dy in range(NY) for dk in range(NK)]
    offs = [o for o in offs if o != (0, 0, 0, 0)]
    return sorted(offs, key=lambda o: (-(dist[o[0]] + dist[o[1]] + dist[o[2]]), -o[3]))


def rates():
    out = []
    for k in range(STEPS):
        t = np.float32(START + 1 + k)
        forget = np.float32(1.0) - np.power(t, np.float32(-0.8))
        out.append((float(forget), float(np.float32(1.0) - forget), float(np.power(t, np.float32(-0.5)))))
    return out


def up(x, n):
    return pltpu.roll(x, 8 - n, 0)


def down(x, n):
    return pltpu.roll(x, n, 0)


def fold8(v):
    s = lax.broadcasted_iota(jnp.int32, (8, 128), 0)
    m4, m2, m1 = s < 4, lax.rem(s, 4) < 2, lax.rem(s, 2) < 1
    w = [jnp.where(m4, v[i], v[i + 4]) + up(jnp.where(m4, v[i + 4], v[i]), 4) for i in range(4)]
    x = [jnp.where(m2, w[i] + up(w[i], 2), w[i + 2] + down(w[i + 2], 2)) for i in range(2)]
    return jnp.where(m1, x[0] + up(x[0], 1), x[1] + down(x[1], 1))


def kernel(
    grad_hbm, param_hbm, row_hbm, col_hbm,
    p, u, factor_ref, newrow_ref, newcol_ref,
    g, row_ref, col_ref, s, s_in, s_sum, xa, za, zb, xb, rowbox, w, w_in, w_sum, wx, wz, c, bbox,
    g_sem, p_sem, col_sem, row_sem, sp_s, sp_r, xa_s, xa_r, za_s, za_r, zb_s, zb_r, xb_s, xb_r,
    box_s, box_r, wp_s, wp_r, wx_s, wx_r, wz_s, wz_r, cx_s, cx_r, cz_s, cz_r, b_s, b_r, sem_b, sem_c, sem_d,
):
    rate = rates()
    row, y = lax.axis_index("row"), lax.axis_index("col")
    z, x, k = lax.div(row, 8), lax.rem(lax.div(row, 2), 4), lax.rem(row, 2)
    zz = [z, *[lax.rem(z + d, NZ) for d in range(1, NZ)]]
    xx = [x, *[lax.rem(x + d, NX) for d in range(1, NX)]]
    yy = [y, *[lax.rem(y + d, NY) for d in range(1, NY)]]
    kk = [k, 1 - k]

    def at(dz=0, dx=0, dy=0, dk=0):
        return (zz[dz] * 8 + xx[dx] * 2 + kk[dk], yy[dy])

    order = (2, 1, 3)
    pair = at(dk=1)
    xs = [at(dx=d) for d in order]
    zs = [at(dz=d) for d in order]
    ys = [at(dy=d) for d in order]

    def signal(sem, devices):
        for d in devices:
            pl.semaphore_signal(sem, inc=1, device_id=d, device_id_type=MESH)

    def remote(src, dst, send, recv, device):
        return pltpu.make_async_remote_copy(src, dst, send, recv, device_id=device, device_id_type=MESH)

    def several(ref, count, send, recv):
        return remote(ref.at[pl.ds(0, count)], ref.at[pl.ds(0, count)], send, recv, pair)

    halves = (1 - k, k)

    def columns(h):
        return pl.ds(pl.multiple_of(halves[h] * HCOLS, 128), HCOLS)

    barrier = pltpu.get_barrier_semaphore()
    g_loads = [pltpu.make_async_copy(grad_hbm.at[:, :, columns(h)], g.at[h], g_sem.at[h]) for h in range(2)]
    p_loads = [pltpu.make_async_copy(param_hbm.at[:, columns(h)], p.at[h], p_sem.at[h]) for h in range(2)]
    col_load = pltpu.make_async_copy(col_hbm.at[pl.ds(pl.multiple_of(k * HALF, 8), HALF)], col_ref, col_sem)
    row_load = pltpu.make_async_copy(row_hbm, row_ref, row_sem)
    g_loads[0].start()
    signal(barrier, [*zs, *xs, *ys, pair])
    for load in (g_loads[1], row_load, col_load, *p_loads):
        load.start()

    lane = lax.broadcasted_iota(jnp.int32, (LROWS, 128), 1)
    sublane = lax.broadcasted_iota(jnp.int32, (LROWS, 128), 0)
    zero = jnp.zeros((8, 128), F32)

    def tile(h, i, n):
        return g[h, i, :, n * 128 : (n + 1) * 128].astype(F32)

    rows = [[None] * 4 for _ in range(STEPS)]

    def squares(h):
        g_loads[h].wait()
        for q in range(PIECES):
            last = []
            for i in range(STEPS):
                sums = []
                for j in range(PTILES):
                    a = tile(h, i, q * PTILES + j)
                    a = a * a
                    rows[i][j % 4] = a if rows[i][j % 4] is None else rows[i][j % 4] + a
                    sums.append(a[:8] + a[8:])
                s[h, q, 8 * i : 8 * i + 8, :] = fold8(sums[:8])
                last.append(sums[8])
            s[h, q, 24:32, :] = fold8(last + [zero] * (8 - STEPS))

    sp_copies = [
        remote(s.at[0, pl.ds(m * 4, 4)], s_in.at[pl.ds(m * 4, 4)], sp_s.at[m], sp_r.at[m], pair) for m in range(2)
    ]
    squares(0)
    pl.semaphore_wait(barrier, 10)
    for copy in sp_copies:
        copy.start()
    signal(sem_b, [pair])
    squares(1)

    packed = jnp.zeros((LROWS, 128), F32)
    for i in range(STEPS):
        total = (rows[i][0] + rows[i][1]) + (rows[i][2] + rows[i][3])
        packed = jnp.where(lane == sublane + LROWS * i, jnp.sum(total, axis=1, keepdims=True), packed)
    rowbox[y] = jnp.sum(packed, axis=0, keepdims=True)
    for d in ys:
        remote(rowbox.at[y], rowbox.at[y], box_s, box_r, d).start()

    def scatter_x(mine, ref, send, recv):
        ref[x] = mine[x]
        for n, d in enumerate(order):
            remote(mine.at[xx[d]], ref.at[x], send, recv, xs[n]).start()

    def scatter_z(mine, ref, send, recv):
        ref[z] = mine[4 + z]
        for n, d in enumerate(order):
            remote(mine.at[4 + zz[d]], ref.at[z], send, recv, zs[n]).start()

    def four(ref):
        return (ref[0] + ref[1]) + (ref[2] + ref[3])

    sp_copies[0].wait_recv()
    for q in range(4):
        s_sum[q] = s[1, q] + s_in[q]
    scatter_x(s_sum, xa, xa_s, xa_r)
    sp_copies[1].wait_recv()
    for q in range(4, 8):
        s_sum[q] = s[1, q] + s_in[q]
    scatter_z(s_sum, za, za_s, za_r)
    pl.semaphore_wait(sem_b, 1)
    signal(sem_c, xs)

    def norm(h):
        def group(n, acc):
            for j in range(8):
                a = p[h, :, pl.ds(pl.multiple_of(n * 1024 + j * 128, 128), 128)]
                a = a * a
                acc = acc + (a[:8] + a[8:])
            return acc

        return group

    psum = zero
    for h in range(2):
        p_loads[h].wait()
        psum = lax.fori_loop(0, HCOLS // 1024, norm(h), psum)
    pl.semaphore_wait(sem_c, 3)
    signal(sem_d, zs)

    several(rowbox, 3, box_s, box_r).wait_recv()
    row_load.wait()
    totals = (rowbox[0] + rowbox[1]) + (rowbox[2] + rowbox[3])
    i0 = lax.broadcasted_iota(jnp.int32, (LROWS, LROWS), 0)
    i1 = lax.broadcasted_iota(jnp.int32, (LROWS, LROWS), 1)
    state = jnp.sum(jnp.where(i0 == i1, row_ref[...], 0.0), axis=1, keepdims=True)
    rr = []
    for i in range(STEPS):
        total = jnp.sum(jnp.where(lane == sublane + LROWS * i, totals, 0.0), axis=1, keepdims=True)
        state = rate[i][0] * state + rate[i][1] * (total / COLS)
        rr.append(jnp.broadcast_to(lax.rsqrt(state), (LROWS, 128)))
    newrow_ref[...] = jnp.sum(jnp.where(i0 == i1, state, 0.0), axis=0, keepdims=True)

    def products(h):
        def piece(q, _):
            sums = [[] for _ in range(PRODUCTS)]
            for j in range(PTILES):
                cols = pl.ds(pl.multiple_of(q * PCOLS + j * 128, 128), 128)
                a = [g[h, i, :, cols].astype(F32) * rr[i] for i in range(STEPS)]
                b = p[h, :, cols]
                for m, v in enumerate((a[0] * a[0], a[1] * a[1], a[2] * a[2], a[0] * a[1], a[0] * b, a[1] * b)):
                    sums[m].append(v[:8] + v[8:])
            for m in range(PRODUCTS):
                w[h, q, 8 * m : 8 * m + 8, :] = fold8(sums[m][:8])
            w[h, q, 48:56, :] = fold8([*[v[8] for v in sums], zero, zero])
            return 0

        return piece

    wp_copies = [
        remote(w.at[0, pl.ds(m * 4, 4)], w_in.at[pl.ds(m * 4, 4)], wp_s.at[m], wp_r.at[m], pair) for m in range(2)
    ]
    for m in range(2):
        lax.fori_loop(m * 4, m * 4 + 4, products(0), 0)
        wp_copies[m].start()

    several(xa, 3, xa_s, xa_r).wait_recv()
    zb[z] = four(xa)
    for d in zs:
        remote(zb.at[z], zb.at[z], zb_s, zb_r, d).start()
    several(za, 3, za_s, za_r).wait_recv()
    xb[x] = four(za)
    for d in xs:
        remote(xb.at[x], xb.at[x], xb_s, xb_r, d).start()
    lax.fori_loop(0, PIECES, products(1), 0)

    wp_copies[0].wait_recv()
    for q in range(4):
        w_sum[q] = w[1, q] + w_in[q]
    scatter_x(w_sum, wx, wx_s, wx_r)
    wp_copies[1].wait_recv()
    for q in range(4, 8):
        w_sum[q] = w[1, q] + w_in[q]
    scatter_z(w_sum, wz, wz_s, wz_r)

    col_load.wait()
    scale = []
    for axis, ref, send, recv, mine in ((0, zb, zb_s, zb_r, x), (1, xb, xb_s, xb_r, z + 4)):
        several(ref, 3, send, recv).wait_recv()
        sums = four(ref)
        first = mine * PTILES
        state8, state1 = col_ref[pl.ds(first, 8), :], col_ref[pl.ds(first + 8, 1), :]
        scale8, scale1 = [], []
        for i in range(STEPS):
            state8 = rate[i][0] * state8 + rate[i][1] * (sums[8 * i : 8 * i + 8] / ROWS)
            state1 = rate[i][0] * state1 + rate[i][1] * (sums[24 + i : 25 + i] / ROWS)
            c[1, mine, 8 * i : 8 * i + 8, :] = state8
            c[1, mine, 24 + i : 25 + i, :] = state1
            scale8.append(lax.rsqrt(state8))
            scale1.append(lax.rsqrt(state1))
        scale.append((scale8, scale1))
        send, recv = (cx_s, cx_r) if axis == 0 else (cz_s, cz_r)
        for dk in (1, 0):
            for d in (*order, 0):
                if d or dk:
                    to = at(dx=d, dk=dk) if axis == 0 else at(dz=d, dk=dk)
                    remote(c.at[1, mine], c.at[1 - dk, mine], send.at[dk], recv.at[dk], to).start()

    acc = [None] * PRODUCTS
    extra = None
    for axis, ref, send, recv in ((0, wx, wx_s, wx_r), (1, wz, wz_s, wz_r)):
        several(ref, 3, send, recv).wait_recv()
        sums = four(ref)
        q8, q1 = scale[axis]
        for m, f in enumerate((q8[0] * q8[0], q8[1] * q8[1], q8[2] * q8[2], q8[0] * q8[1], q8[0], q8[1])):
            v = f * sums[8 * m : 8 * m + 8]
            acc[m] = v if axis == 0 else acc[m] + v
        f = (q1[0] * q1[0], q1[1] * q1[1], q1[2] * q1[2], q1[0] * q1[1], q1[0], q1[1], q1[0] * 0.0, q1[0] * 0.0)
        v = jnp.concatenate(f, axis=0) * sums[48:56]
        extra = v if axis == 0 else extra + v
    sums = jnp.sum(fold8([*acc, psum, zero]) + extra, axis=1, keepdims=True)
    j0 = lax.broadcasted_iota(jnp.int32, (8, 128), 0)
    j1 = lax.broadcasted_iota(jnp.int32, (8, 128), 1)
    me = y * NROW + row
    bbox[me] = jnp.sum(jnp.where(j0 == j1, sums, 0.0), axis=0, keepdims=True)
    pl.semaphore_wait(sem_d, 3)
    for off in far_first():
        remote(bbox.at[me], bbox.at[me], b_s, b_r, at(*off)).start()

    def updates(h):
        def piece(q, _):
            scales = lax.rsqrt(c[h, q])
            for j in range(PTILES):
                cols = pl.ds(pl.multiple_of(q * PCOLS + j * 128, 128), 128)
                for i in range(STEPS):
                    at_row = 8 * i + j if j < 8 else 24 + i
                    u[h, i, :, cols] = g[h, i, :, cols].astype(F32) * rr[i] * scales[at_row : at_row + 1]
            return 0

        return piece

    for h in (1, 0):
        count = 3 if h else 4
        several(c.at[h], count, cx_s.at[1 - h], cx_r.at[1 - h]).wait_recv()
        several(c.at[h], count, cz_s.at[1 - h], cz_r.at[1 - h]).wait_recv()
        lax.fori_loop(0, PIECES, updates(h), 0)
        for q in range(PIECES):
            newcol_ref[h, q * PTILES : q * PTILES + 8, :] = c[h, q, 16:24, :]
            newcol_ref[h, q * PTILES + 8 : q * PTILES + 9, :] = c[h, q, 26:27, :]

    several(bbox, NALL - 1, b_s, b_r).wait_recv()
    sums = jnp.sum(bbox[...], axis=0)
    j1 = lax.broadcasted_iota(jnp.int32, (1, 128), 1)
    uu0, uu1, uu2, u01, pu0, pu1, pp = [
        jnp.sum(jnp.where(j1 == m, sums, 0.0), axis=1, keepdims=True) for m in range(7)
    ]
    count = float(ROWS * COLS)
    clip = [jnp.maximum(1.0, jnp.sqrt(v / count)) for v in (uu0, uu1, uu2)]
    f0 = rate[0][2] * jnp.sqrt(pp / count) / clip[0]
    pp = pp - 2.0 * f0 * pu0 + f0 * f0 * uu0
    f1 = rate[1][2] * jnp.sqrt(pp / count) / clip[1]
    pp = pp - 2.0 * f1 * (pu1 - f0 * u01) + f1 * f1 * uu1
    f2 = rate[2][2] * jnp.sqrt(pp / count) / clip[2]
    for i, v in enumerate((f0, f1, f2)):
        factor_ref[i] = jnp.broadcast_to(v, (8, 128))

    for copy in (*sp_copies, *wp_copies):
        copy.wait_send()
    for ref, send, recv in (
        (xa, xa_s, xa_r), (za, za_s, za_r), (zb, zb_s, zb_r), (xb, xb_s, xb_r),
        (rowbox, box_s, box_r), (wx, wx_s, wx_r), (wz, wz_s, wz_r),
    ):
        several(ref, 3, send, recv).wait_send()
    for dk in range(2):
        several(c.at[0], 3 + dk, cx_s.at[dk], cx_r.at[dk]).wait_send()
        several(c.at[0], 3 + dk, cz_s.at[dk], cz_r.at[dk]).wait_send()
    several(bbox, NALL - 1, b_s, b_r).wait_send()


def finish(p, u, factor_ref, newrow_ref, newcol_ref, out_hbm, row_hbm, col_hbm, o, out_sem, row_sem, col_sem):
    k = lax.rem(lax.axis_index("row"), 2)
    halves = (1 - k, k)
    outs = [pltpu.make_async_copy(newrow_ref, row_hbm, row_sem)]
    for h in range(2):
        tiles = pl.ds(pl.multiple_of(halves[h] * HALF, 8), HALF)
        outs.append(pltpu.make_async_copy(newcol_ref.at[h], col_hbm.at[tiles], col_sem.at[h]))
    for out in outs:
        out.start()
    f = [jnp.concatenate([factor_ref[i], factor_ref[i]], axis=0) for i in range(STEPS)]
    width = HCOLS // OUT_PARTS
    for h in range(2):
        for part in range(OUT_PARTS):
            for n in range(width // 128):
                cols = pl.ds(part * width + n * 128, 128)
                a = p[h, :, cols] - f[0] * u[h, 0, :, cols]
                o[h, :, cols] = a - (f[1] * u[h, 1, :, cols] + f[2] * u[h, 2, :, cols])
            src = o.at[h, :, pl.ds(part * width, width)]
            dst = out_hbm.at[:, pl.ds(pl.multiple_of(halves[h] * HCOLS + part * width, 128), width)]
            outs.append(pltpu.make_async_copy(src, dst, out_sem.at[h, part]))
            outs[-1].start()
    for out in outs:
        out.wait()


def local(gradients, parameter, row_state, col_state):
    args = (gradients, parameter, row_state.reshape(1, LROWS), col_state.reshape(TILES, 128))
    vmem = pl.BlockSpec(memory_space=pltpu.VMEM)
    hbm = pl.BlockSpec(memory_space=pltpu.HBM)
    dma = pltpu.SemaphoreType.DMA
    two = dma((2,))
    state = pl.pallas_call(
        kernel,
        name="exchange",
        out_shape=(
            jax.ShapeDtypeStruct((2, LROWS, HCOLS), F32),
            jax.ShapeDtypeStruct((2, STEPS, LROWS, HCOLS), F32),
            jax.ShapeDtypeStruct((STEPS, 8, 128), F32),
            jax.ShapeDtypeStruct((1, LROWS), F32),
            jax.ShapeDtypeStruct((2, HALF, 128), F32),
        ),
        in_specs=[hbm] * 4,
        out_specs=(vmem,) * 5,
        scratch_shapes=[
            pltpu.VMEM((2, STEPS, LROWS, HCOLS), jnp.bfloat16),
            pltpu.VMEM((1, LROWS), F32),
            pltpu.VMEM((HALF, 128), F32),
            pltpu.VMEM((2, PIECES, SROWS, 128), F32),
            pltpu.VMEM((PIECES, SROWS, 128), F32),
            pltpu.VMEM((PIECES, SROWS, 128), F32),
            pltpu.VMEM((NX, SROWS, 128), F32),
            pltpu.VMEM((NZ, SROWS, 128), F32),
            pltpu.VMEM((NZ, SROWS, 128), F32),
            pltpu.VMEM((NX, SROWS, 128), F32),
            pltpu.VMEM((NY, 1, 128), F32),
            pltpu.VMEM((2, PIECES, WROWS, 128), F32),
            pltpu.VMEM((PIECES, WROWS, 128), F32),
            pltpu.VMEM((PIECES, WROWS, 128), F32),
            pltpu.VMEM((NX, WROWS, 128), F32),
            pltpu.VMEM((NZ, WROWS, 128), F32),
            pltpu.VMEM((2, PIECES, SROWS, 128), F32),
            pltpu.VMEM((NALL, 1, 128), F32),
            two, two, dma, dma, two, two, dma, dma, dma, dma, dma, dma, dma, dma,
            dma, dma, two, two, dma, dma, dma, dma, two, two, two, two, dma, dma,
            pltpu.SemaphoreType.REGULAR, pltpu.SemaphoreType.REGULAR, pltpu.SemaphoreType.REGULAR,
        ],
        compiler_params=pltpu.CompilerParams(
            collective_id=0, has_side_effects=True, vmem_limit_bytes=40 * 2**20
        ),
        cost_estimate=pl.CostEstimate(flops=20_000_000, bytes_accessed=4_200_000, transcendentals=100_000),
    )(*[pltpu.with_memory_space_constraint(a, pltpu.HBM) for a in args])
    new_param, new_row, new_col = pl.pallas_call(
        finish,
        name="finish",
        out_shape=(
            jax.ShapeDtypeStruct((LROWS, LCOLS), F32),
            jax.ShapeDtypeStruct((1, LROWS), F32),
            jax.ShapeDtypeStruct((TILES, 128), F32),
        ),
        in_specs=[vmem] * 5,
        out_specs=(hbm,) * 3,
        scratch_shapes=[pltpu.VMEM((2, LROWS, HCOLS), F32), dma((2, OUT_PARTS)), dma, dma((2,))],
        compiler_params=pltpu.CompilerParams(vmem_limit_bytes=40 * 2**20),
        cost_estimate=pl.CostEstimate(flops=2_000_000, bytes_accessed=1_200_000, transcendentals=0),
    )(*state)
    return new_param, new_row.reshape(LROWS), new_col.reshape(LCOLS)


def solution(mesh):
    placed = (P(None, "row", "col"), P("row", "col"), P("row"), P("col"))
    return jax.shard_map(
        local,
        mesh=mesh,
        in_specs=placed,
        out_specs=(P("row", "col"), P("row"), P("col")),
        check_vma=False,
    )
```

```python
import functools

import jax
import jax.numpy as jnp
import numpy as np
from jax import lax
from jax.experimental import pallas as pl
from jax.experimental.pallas import tpu as pltpu
from jax.sharding import PartitionSpec as P

MESH = pl.DeviceIdType.MESH
START = 100
F32 = jnp.float32

NZ, NX, NK, NY = 4, 4, 2, 4
NROW, NALL = NZ * NX * NK, NZ * NX * NK * NY
STEPS, LROWS, LCOLS = 3, 16, 18432
ROWS, COLS = LROWS * NROW, LCOLS * NY
TILES = LCOLS // 128
HALF, HCOLS = TILES // 2, LCOLS // 2
PIECES = 8
PTILES = HALF // PIECES
PCOLS = PTILES * 128
SROWS = 32
WROWS = 56
PRODUCTS = 6
OUT_PARTS = 3


def far_first():
    dist = (0, 1, 2, 1)
    offs = [(dz, dx, dy, dk) for dz in range(NZ) for dx in range(NX) for dy in range(NY) for dk in range(NK)]
    offs = [o for o in offs if o != (0, 0, 0, 0)]
    return sorted(offs, key=lambda o: (-(dist[o[0]] + dist[o[1]] + dist[o[2]]), -o[3]))


def rates():
    out = []
    for k in range(STEPS):
        t = np.float32(START + 1 + k)
        forget = np.float32(1.0) - np.power(t, np.float32(-0.8))
        out.append((float(forget), float(np.float32(1.0) - forget), float(np.power(t, np.float32(-0.5)))))
    return out


def up(x, n):
    return pltpu.roll(x, 8 - n, 0)


def down(x, n):
    return pltpu.roll(x, n, 0)


def fold8(v):
    s = lax.broadcasted_iota(jnp.int32, (8, 128), 0)
    m4, m2, m1 = s < 4, lax.rem(s, 4) < 2, lax.rem(s, 2) < 1
    w = [jnp.where(m4, v[i], v[i + 4]) + up(jnp.where(m4, v[i + 4], v[i]), 4) for i in range(4)]
    x = [jnp.where(m2, w[i] + up(w[i], 2), w[i + 2] + down(w[i + 2], 2)) for i in range(2)]
    return jnp.where(m1, x[0] + up(x[0], 1), x[1] + down(x[1], 1))


def kernel(
    grad_hbm, param_hbm, row_hbm, col_hbm,
    p, u, factor_ref, newrow_ref, newcol_ref,
    g, row_ref, col_ref, s, s_in, s_sum, xa, za, zb, xb, rowbox, w, w_in, w_sum, wx, wz, c, bbox,
    g_sem, p_sem, col_sem, row_sem, sp_s, sp_r, xa_s, xa_r, za_s, za_r, zb_s, zb_r, xb_s, xb_r,
    box_s, box_r, wp_s, wp_r, wx_s, wx_r, wz_s, wz_r, cx_s, cx_r, cz_s, cz_r, cp_s, cp_r, b_s, b_r, sem_p, sem_q, sem_c, sem_d,
):
    rate = rates()
    row, y = lax.axis_index("row"), lax.axis_index("col")
    z, x, k = lax.div(row, 8), lax.rem(lax.div(row, 2), 4), lax.rem(row, 2)
    zz = [z, *[lax.rem(z + d, NZ) for d in range(1, NZ)]]
    xx = [x, *[lax.rem(x + d, NX) for d in range(1, NX)]]
    yy = [y, *[lax.rem(y + d, NY) for d in range(1, NY)]]
    kk = [k, 1 - k]

    def at(dz=0, dx=0, dy=0, dk=0):
        return (zz[dz] * 8 + xx[dx] * 2 + kk[dk], yy[dy])

    order = (2, 1, 3)
    pair = at(dk=1)
    xs = [at(dx=d) for d in order]
    zs = [at(dz=d) for d in order]
    ys = [at(dy=d) for d in order]

    def signal(sem, devices):
        for d in devices:
            pl.semaphore_signal(sem, inc=1, device_id=d, device_id_type=MESH)

    def remote(src, dst, send, recv, device):
        return pltpu.make_async_remote_copy(src, dst, send, recv, device_id=device, device_id_type=MESH)

    def several(ref, count, send, recv):
        return remote(ref.at[pl.ds(0, count)], ref.at[pl.ds(0, count)], send, recv, pair)

    halves = (1 - k, k)

    def columns(h):
        return pl.ds(pl.multiple_of(halves[h] * HCOLS, 128), HCOLS)

    barrier = pltpu.get_barrier_semaphore()
    g_loads = [pltpu.make_async_copy(grad_hbm.at[:, :, columns(h)], g.at[h], g_sem.at[h]) for h in range(2)]
    p_loads = [pltpu.make_async_copy(param_hbm.at[:, columns(h)], p.at[h], p_sem.at[h]) for h in range(2)]
    col_load = pltpu.make_async_copy(col_hbm.at[pl.ds(pl.multiple_of(k * HALF, 8), HALF)], col_ref, col_sem)
    row_load = pltpu.make_async_copy(row_hbm, row_ref, row_sem)
    g_loads[0].start()
    signal(barrier, [(d[0] - k, d[1]) for d in (*zs, *xs, *ys)])

    @pl.when(k == 0)
    def _():
        signal(barrier, [pair])

    for load in (g_loads[1], row_load, col_load, *p_loads):
        load.start()

    lane = lax.broadcasted_iota(jnp.int32, (LROWS, 128), 1)
    sublane = lax.broadcasted_iota(jnp.int32, (LROWS, 128), 0)
    zero = jnp.zeros((8, 128), F32)

    def tile(h, i, n):
        return g[h, i, :, n * 128 : (n + 1) * 128].astype(F32)

    rows = [[None] * 4 for _ in range(STEPS)]

    def squares(h):
        g_loads[h].wait()
        for q in range(PIECES):
            last = []
            for i in range(STEPS):
                sums = []
                for j in range(PTILES):
                    a = tile(h, i, q * PTILES + j)
                    a = a * a
                    rows[i][j % 4] = a if rows[i][j % 4] is None else rows[i][j % 4] + a
                    sums.append(a[:8] + a[8:])
                s[h, q, 8 * i : 8 * i + 8, :] = fold8(sums[:8])
                last.append(sums[8])
            s[h, q, 24:32, :] = fold8(last + [zero] * (8 - STEPS))

    sp_copies = [
        remote(s.at[0, pl.ds(m * 4, 4)], s_in.at[pl.ds(m * 4, 4)], sp_s.at[m], sp_r.at[m], pair) for m in range(2)
    ]
    squares(0)

    @pl.when(k == 1)
    def _():
        pl.semaphore_wait(barrier, 1)
        signal(sem_p, [pair])

    @pl.when(k == 0)
    def _():
        pl.semaphore_wait(sem_p, 1)

    for copy in sp_copies:
        copy.start()
    squares(1)

    packed = jnp.zeros((LROWS, 128), F32)
    for i in range(STEPS):
        total = (rows[i][0] + rows[i][1]) + (rows[i][2] + rows[i][3])
        packed = jnp.where(lane == sublane + LROWS * i, jnp.sum(total, axis=1, keepdims=True), packed)
    rowbox[y] = jnp.sum(packed, axis=0, keepdims=True)

    @pl.when(k == 0)
    def _():
        pl.semaphore_wait(barrier, 18)
        signal(sem_q, [pair])

    @pl.when(k == 1)
    def _():
        pl.semaphore_wait(sem_q, 1)

    for d in ys:
        remote(rowbox.at[y], rowbox.at[y], box_s, box_r, d).start()

    def scatter_x(mine, ref, send, recv):
        ref[x] = mine[x]
        for n, d in enumerate(order):
            remote(mine.at[xx[d]], ref.at[x], send, recv, xs[n]).start()

    def scatter_z(mine, ref, send, recv):
        ref[z] = mine[4 + z]
        for n, d in enumerate(order):
            remote(mine.at[4 + zz[d]], ref.at[z], send, recv, zs[n]).start()

    def four(ref):
        return (ref[0] + ref[1]) + (ref[2] + ref[3])

    sp_copies[0].wait_recv()
    for q in range(4):
        s_sum[q] = s[1, q] + s_in[q]
    scatter_x(s_sum, xa, xa_s, xa_r)
    sp_copies[1].wait_recv()
    for q in range(4, 8):
        s_sum[q] = s[1, q] + s_in[q]
    scatter_z(s_sum, za, za_s, za_r)
    signal(sem_c, xs)

    def norm(h):
        def group(n, acc):
            for j in range(8):
                a = p[h, :, pl.ds(pl.multiple_of(n * 1024 + j * 128, 128), 128)]
                a = a * a
                acc = acc + (a[:8] + a[8:])
            return acc

        return group

    psum = zero
    for h in range(2):
        p_loads[h].wait()
        psum = lax.fori_loop(0, HCOLS // 1024, norm(h), psum)
    pl.semaphore_wait(sem_c, 3)
    signal(sem_d, zs)

    several(rowbox, 3, box_s, box_r).wait_recv()
    row_load.wait()
    totals = (rowbox[0] + rowbox[1]) + (rowbox[2] + rowbox[3])
    i0 = lax.broadcasted_iota(jnp.int32, (LROWS, LROWS), 0)
    i1 = lax.broadcasted_iota(jnp.int32, (LROWS, LROWS), 1)
    state = jnp.sum(jnp.where(i0 == i1, row_ref[...], 0.0), axis=1, keepdims=True)
    rr = []
    for i in range(STEPS):
        total = jnp.sum(jnp.where(lane == sublane + LROWS * i, totals, 0.0), axis=1, keepdims=True)
        state = rate[i][0] * state + rate[i][1] * (total / COLS)
        rr.append(jnp.broadcast_to(lax.rsqrt(state), (LROWS, 128)))
    newrow_ref[...] = jnp.sum(jnp.where(i0 == i1, state, 0.0), axis=0, keepdims=True)

    def products(h):
        def piece(q, _):
            sums = [[] for _ in range(PRODUCTS)]
            for j in range(PTILES):
                cols = pl.ds(pl.multiple_of(q * PCOLS + j * 128, 128), 128)
                a = [g[h, i, :, cols].astype(F32) * rr[i] for i in range(STEPS)]
                b = p[h, :, cols]
                for m, v in enumerate((a[0] * a[0], a[1] * a[1], a[2] * a[2], a[0] * a[1], a[0] * b, a[1] * b)):
                    sums[m].append(v[:8] + v[8:])
            for m in range(PRODUCTS):
                w[h, q, 8 * m : 8 * m + 8, :] = fold8(sums[m][:8])
            w[h, q, 48:56, :] = fold8([*[v[8] for v in sums], zero, zero])
            return 0

        return piece

    wp_copies = [
        remote(w.at[0, pl.ds(m * 4, 4)], w_in.at[pl.ds(m * 4, 4)], wp_s.at[m], wp_r.at[m], pair) for m in range(2)
    ]
    for m in range(2):
        lax.fori_loop(m * 4, m * 4 + 4, products(0), 0)
        wp_copies[m].start()

    several(xa, 3, xa_s, xa_r).wait_recv()
    zb[z] = four(xa)
    for d in zs:
        remote(zb.at[z], zb.at[z], zb_s, zb_r, d).start()
    several(za, 3, za_s, za_r).wait_recv()
    xb[x] = four(za)
    for d in xs:
        remote(xb.at[x], xb.at[x], xb_s, xb_r, d).start()

    lax.fori_loop(0, 4, products(1), 0)
    wp_copies[0].wait_recv()
    for q in range(4):
        w_sum[q] = w[1, q] + w_in[q]
    scatter_x(w_sum, wx, wx_s, wx_r)
    lax.fori_loop(4, 8, products(1), 0)
    wp_copies[1].wait_recv()
    for q in range(4, 8):
        w_sum[q] = w[1, q] + w_in[q]
    scatter_z(w_sum, wz, wz_s, wz_r)

    col_load.wait()
    scale = []
    for axis, ref, send, recv, mine in ((0, zb, zb_s, zb_r, x), (1, xb, xb_s, xb_r, z + 4)):
        several(ref, 3, send, recv).wait_recv()
        sums = four(ref)
        first = mine * PTILES
        state8, state1 = col_ref[pl.ds(first, 8), :], col_ref[pl.ds(first + 8, 1), :]
        scale8, scale1 = [], []
        for i in range(STEPS):
            state8 = rate[i][0] * state8 + rate[i][1] * (sums[8 * i : 8 * i + 8] / ROWS)
            state1 = rate[i][0] * state1 + rate[i][1] * (sums[24 + i : 25 + i] / ROWS)
            c[1, mine, 8 * i : 8 * i + 8, :] = state8
            c[1, mine, 24 + i : 25 + i, :] = state1
            scale8.append(lax.rsqrt(state8))
            scale1.append(lax.rsqrt(state1))
        scale.append((scale8, scale1))
        send, recv, to = (cx_s, cx_r, xs) if axis == 0 else (cz_s, cz_r, zs)
        for d in to:
            remote(c.at[1, mine], c.at[1, mine], send, recv, d).start()

    acc = [None] * PRODUCTS
    extra = None
    for axis, ref, send, recv in ((0, wx, wx_s, wx_r), (1, wz, wz_s, wz_r)):
        several(ref, 3, send, recv).wait_recv()
        sums = four(ref)
        q8, q1 = scale[axis]
        for m, f in enumerate((q8[0] * q8[0], q8[1] * q8[1], q8[2] * q8[2], q8[0] * q8[1], q8[0], q8[1])):
            v = f * sums[8 * m : 8 * m + 8]
            acc[m] = v if axis == 0 else acc[m] + v
        f = (q1[0] * q1[0], q1[1] * q1[1], q1[2] * q1[2], q1[0] * q1[1], q1[0], q1[1], q1[0] * 0.0, q1[0] * 0.0)
        v = jnp.concatenate(f, axis=0) * sums[48:56]
        extra = v if axis == 0 else extra + v
    sums = jnp.sum(fold8([*acc, psum, zero]) + extra, axis=1, keepdims=True)
    j0 = lax.broadcasted_iota(jnp.int32, (8, 128), 0)
    j1 = lax.broadcasted_iota(jnp.int32, (8, 128), 1)
    me = y * NROW + row
    bbox[me] = jnp.sum(jnp.where(j0 == j1, sums, 0.0), axis=0, keepdims=True)
    pl.semaphore_wait(sem_d, 3)
    for off in far_first():
        remote(bbox.at[me], bbox.at[me], b_s, b_r, at(*off)).start()

    def updates(h):
        def piece(q, _):
            scales = lax.rsqrt(c[h, q])
            for j in range(PTILES):
                cols = pl.ds(pl.multiple_of(q * PCOLS + j * 128, 128), 128)
                for i in range(STEPS):
                    at_row = 8 * i + j if j < 8 else 24 + i
                    u[h, i, :, cols] = g[h, i, :, cols].astype(F32) * rr[i] * scales[at_row : at_row + 1]
            return 0

        return piece

    c_copy = remote(c.at[1], c.at[0], cp_s, cp_r, pair)
    several(c.at[1], 3, cx_s, cx_r).wait_recv()
    several(c.at[1], 3, cz_s, cz_r).wait_recv()
    c_copy.start()
    for h in (1, 0):
        if h == 0:
            c_copy.wait_recv()
        lax.fori_loop(0, PIECES, updates(h), 0)
        for q in range(PIECES):
            newcol_ref[h, q * PTILES : q * PTILES + 8, :] = c[h, q, 16:24, :]
            newcol_ref[h, q * PTILES + 8 : q * PTILES + 9, :] = c[h, q, 26:27, :]

    for copy in (*sp_copies, *wp_copies, c_copy):
        copy.wait_send()
    for ref, send, recv in (
        (xa, xa_s, xa_r), (za, za_s, za_r), (zb, zb_s, zb_r), (xb, xb_s, xb_r),
        (rowbox, box_s, box_r), (wx, wx_s, wx_r), (wz, wz_s, wz_r),
        (c.at[1], cx_s, cx_r), (c.at[1], cz_s, cz_r),
    ):
        several(ref, 3, send, recv).wait_send()

    several(bbox, NALL - 1, b_s, b_r).wait_recv()
    sums = jnp.sum(bbox[...], axis=0)
    j1 = lax.broadcasted_iota(jnp.int32, (1, 128), 1)
    uu0, uu1, uu2, u01, pu0, pu1, pp = [
        jnp.sum(jnp.where(j1 == m, sums, 0.0), axis=1, keepdims=True) for m in range(7)
    ]
    count = float(ROWS * COLS)
    clip = [jnp.maximum(1.0, jnp.sqrt(v / count)) for v in (uu0, uu1, uu2)]
    f0 = rate[0][2] * jnp.sqrt(pp / count) / clip[0]
    pp = pp - 2.0 * f0 * pu0 + f0 * f0 * uu0
    f1 = rate[1][2] * jnp.sqrt(pp / count) / clip[1]
    pp = pp - 2.0 * f1 * (pu1 - f0 * u01) + f1 * f1 * uu1
    f2 = rate[2][2] * jnp.sqrt(pp / count) / clip[2]
    for i, v in enumerate((f0, f1, f2)):
        factor_ref[i] = jnp.broadcast_to(v, (8, 128))

    several(bbox, NALL - 1, b_s, b_r).wait_send()


def finish(p, u, factor_ref, newrow_ref, newcol_ref, out_hbm, row_hbm, col_hbm, o, out_sem, row_sem, col_sem):
    k = lax.rem(lax.axis_index("row"), 2)
    halves = (1 - k, k)
    outs = [pltpu.make_async_copy(newrow_ref, row_hbm, row_sem)]
    for h in range(2):
        tiles = pl.ds(pl.multiple_of(halves[h] * HALF, 8), HALF)
        outs.append(pltpu.make_async_copy(newcol_ref.at[h], col_hbm.at[tiles], col_sem.at[h]))
    for out in outs:
        out.start()
    f = [jnp.concatenate([factor_ref[i], factor_ref[i]], axis=0) for i in range(STEPS)]
    width = HCOLS // OUT_PARTS
    for h in range(2):
        for part in range(OUT_PARTS):
            for n in range(width // 128):
                cols = pl.ds(part * width + n * 128, 128)
                a = p[h, :, cols] - f[0] * u[h, 0, :, cols]
                o[h, :, cols] = a - (f[1] * u[h, 1, :, cols] + f[2] * u[h, 2, :, cols])
            src = o.at[h, :, pl.ds(part * width, width)]
            dst = out_hbm.at[:, pl.ds(pl.multiple_of(halves[h] * HCOLS + part * width, 128), width)]
            outs.append(pltpu.make_async_copy(src, dst, out_sem.at[h, part]))
            outs[-1].start()
    for out in outs:
        out.wait()


def local(gradients, parameter, row_state, col_state):
    args = (gradients, parameter, row_state.reshape(1, LROWS), col_state.reshape(TILES, 128))
    vmem = pl.BlockSpec(memory_space=pltpu.VMEM)
    hbm = pl.BlockSpec(memory_space=pltpu.HBM)
    dma = pltpu.SemaphoreType.DMA
    regular, two = pltpu.SemaphoreType.REGULAR, dma((2,))
    state = pl.pallas_call(
        kernel,
        name="exchange",
        out_shape=(
            jax.ShapeDtypeStruct((2, LROWS, HCOLS), F32),
            jax.ShapeDtypeStruct((2, STEPS, LROWS, HCOLS), F32),
            jax.ShapeDtypeStruct((STEPS, 8, 128), F32),
            jax.ShapeDtypeStruct((1, LROWS), F32),
            jax.ShapeDtypeStruct((2, HALF, 128), F32),
        ),
        in_specs=[hbm] * 4,
        out_specs=(vmem,) * 5,
        scratch_shapes=[
            pltpu.VMEM((2, STEPS, LROWS, HCOLS), jnp.bfloat16),
            pltpu.VMEM((1, LROWS), F32),
            pltpu.VMEM((HALF, 128), F32),
            pltpu.VMEM((2, PIECES, SROWS, 128), F32),
            pltpu.VMEM((PIECES, SROWS, 128), F32),
            pltpu.VMEM((PIECES, SROWS, 128), F32),
            pltpu.VMEM((NX, SROWS, 128), F32),
            pltpu.VMEM((NZ, SROWS, 128), F32),
            pltpu.VMEM((NZ, SROWS, 128), F32),
            pltpu.VMEM((NX, SROWS, 128), F32),
            pltpu.VMEM((NY, 1, 128), F32),
            pltpu.VMEM((2, PIECES, WROWS, 128), F32),
            pltpu.VMEM((PIECES, WROWS, 128), F32),
            pltpu.VMEM((PIECES, WROWS, 128), F32),
            pltpu.VMEM((NX, WROWS, 128), F32),
            pltpu.VMEM((NZ, WROWS, 128), F32),
            pltpu.VMEM((2, PIECES, SROWS, 128), F32),
            pltpu.VMEM((NALL, 1, 128), F32),
            two, two, dma, dma, two, two, dma, dma, dma, dma, dma, dma, dma, dma,
            dma, dma, two, two, dma, dma, dma, dma, dma, dma, dma, dma, dma, dma, dma, dma,
            regular, regular, regular, regular,
        ],
        compiler_params=pltpu.CompilerParams(
            collective_id=0, has_side_effects=True, vmem_limit_bytes=40 * 2**20
        ),
        cost_estimate=pl.CostEstimate(flops=20_000_000, bytes_accessed=4_200_000, transcendentals=100_000),
    )(*[pltpu.with_memory_space_constraint(a, pltpu.HBM) for a in args])
    new_param, new_row, new_col = pl.pallas_call(
        finish,
        name="finish",
        out_shape=(
            jax.ShapeDtypeStruct((LROWS, LCOLS), F32),
            jax.ShapeDtypeStruct((1, LROWS), F32),
            jax.ShapeDtypeStruct((TILES, 128), F32),
        ),
        in_specs=[vmem] * 5,
        out_specs=(hbm,) * 3,
        scratch_shapes=[pltpu.VMEM((2, LROWS, HCOLS), F32), dma((2, OUT_PARTS)), dma, dma((2,))],
        compiler_params=pltpu.CompilerParams(vmem_limit_bytes=40 * 2**20),
        cost_estimate=pl.CostEstimate(flops=2_000_000, bytes_accessed=1_200_000, transcendentals=0),
    )(*state)
    return new_param, new_row.reshape(LROWS), new_col.reshape(LCOLS)


def solution(mesh):
    placed = (P(None, "row", "col"), P("row", "col"), P("row"), P("col"))
    return jax.shard_map(
        local,
        mesh=mesh,
        in_specs=placed,
        out_specs=(P("row", "col"), P("row"), P("col")),
        check_vma=False,
    )
```

```python
import functools

import jax
import jax.numpy as jnp
import numpy as np
from jax import lax
from jax.experimental import pallas as pl
from jax.experimental.pallas import tpu as pltpu
from jax.sharding import PartitionSpec as P

MESH = pl.DeviceIdType.MESH
START = 100
F32 = jnp.float32

NZ, NX, NK, NY = 4, 4, 2, 4
NROW, NALL = NZ * NX * NK, NZ * NX * NK * NY
STEPS, LROWS, LCOLS = 3, 16, 18432
ROWS, COLS = LROWS * NROW, LCOLS * NY
TILES = LCOLS // 128
HALF, HCOLS = TILES // 2, LCOLS // 2
PIECES = 8
PTILES = HALF // PIECES
PCOLS = PTILES * 128
SROWS = 32
WROWS = 56
PRODUCTS = 6
SENT = 2 * PIECES * SROWS + PIECES * WROWS + 6 * (3 * SROWS + WROWS) + NY - 1 + NALL - 1
LOADED = LROWS * TILES + HALF
OUT_PARTS = 3


def far_first():
    dist = (0, 1, 2, 1)
    offs = [(dz, dx, dy, dk) for dz in range(NZ) for dx in range(NX) for dy in range(NY) for dk in range(NK)]
    offs = [o for o in offs if o != (0, 0, 0, 0)]
    return sorted(offs, key=lambda o: (-(dist[o[0]] + dist[o[1]] + dist[o[2]]), -o[3]))


def rates():
    out = []
    for k in range(STEPS):
        t = np.float32(START + 1 + k)
        forget = np.float32(1.0) - np.power(t, np.float32(-0.8))
        out.append((float(forget), float(np.float32(1.0) - forget), float(np.power(t, np.float32(-0.5)))))
    return out


def up(x, n):
    return pltpu.roll(x, 8 - n, 0)


def down(x, n):
    return pltpu.roll(x, n, 0)


def fold8(v):
    s = lax.broadcasted_iota(jnp.int32, (8, 128), 0)
    m4, m2, m1 = s < 4, lax.rem(s, 4) < 2, lax.rem(s, 2) < 1
    w = [jnp.where(m4, v[i], v[i + 4]) + up(jnp.where(m4, v[i + 4], v[i]), 4) for i in range(4)]
    x = [jnp.where(m2, w[i] + up(w[i], 2), w[i + 2] + down(w[i + 2], 2)) for i in range(2)]
    return jnp.where(m1, x[0] + up(x[0], 1), x[1] + down(x[1], 1))


def kernel(
    grad_hbm, param_hbm, row_hbm, col_hbm,
    p, u, factor_ref, newrow_ref, newcol_ref,
    g, row_ref, col_ref, s, s_in, s_sum, r1, r2, rowbox, w, w_in, w_sum, wr, c, bbox, loaded, sent,
    g_sem, row_sem, load_sem, send, sp_r, r1_r, r2_r, box_r, wp_r, wr_r, c_r, cp_r, b_r, sem_p, sem_c, sem_d,
):
    rate = rates()
    row, y = lax.axis_index("row"), lax.axis_index("col")
    z, x, k = lax.div(row, 8), lax.rem(lax.div(row, 2), 4), lax.rem(row, 2)
    zz = [z, *[lax.rem(z + d, NZ) for d in range(1, NZ)]]
    xx = [x, *[lax.rem(x + d, NX) for d in range(1, NX)]]
    yy = [y, *[lax.rem(y + d, NY) for d in range(1, NY)]]
    kk = [k, 1 - k]

    def at(dz=0, dx=0, dy=0, dk=0):
        return (zz[dz] * 8 + xx[dx] * 2 + kk[dk], yy[dy])

    order = (2, 1, 3)
    pair = at(dk=1)
    xs = [at(dx=d) for d in order]
    zs = [at(dz=d) for d in order]
    ys = [at(dy=d) for d in order]

    def signal(sem, devices):
        for d in devices:
            pl.semaphore_signal(sem, inc=1, device_id=d, device_id_type=MESH)

    def remote(src, dst, recv, device):
        return pltpu.make_async_remote_copy(src, dst, send, recv, device_id=device, device_id_type=MESH)

    def several(ref, count, recv):
        return remote(ref.at[pl.ds(0, count)], ref.at[pl.ds(0, count)], recv, pair)

    halves = (1 - k, k)

    def columns(h):
        return pl.ds(pl.multiple_of(halves[h] * HCOLS, 128), HCOLS)

    barrier = pltpu.get_barrier_semaphore()
    g_loads = [pltpu.make_async_copy(grad_hbm.at[:, :, columns(h)], g.at[h], g_sem.at[h]) for h in range(2)]
    p_loads = [pltpu.make_async_copy(param_hbm.at[:, columns(h)], p.at[h], load_sem) for h in range(2)]
    col_load = pltpu.make_async_copy(col_hbm.at[pl.ds(pl.multiple_of(k * HALF, 8), HALF)], col_ref, load_sem)
    row_load = pltpu.make_async_copy(row_hbm, row_ref, row_sem)
    g_loads[0].start()
    signal(barrier, [(d[0] - k, d[1]) for d in (*zs, *xs, *ys)])

    @pl.when(k == 0)
    def _():
        signal(barrier, [pair])

    for load in (g_loads[1], row_load, col_load, *p_loads):
        load.start()

    lane = lax.broadcasted_iota(jnp.int32, (LROWS, 128), 1)
    sublane = lax.broadcasted_iota(jnp.int32, (LROWS, 128), 0)
    zero = jnp.zeros((8, 128), F32)

    def tile(h, i, n):
        return g[h, i, :, n * 128 : (n + 1) * 128].astype(F32)

    rows = [[None] * 4 for _ in range(STEPS)]

    def squares(h):
        g_loads[h].wait()
        for q in range(PIECES):
            last = []
            for i in range(STEPS):
                sums = []
                for j in range(PTILES):
                    a = tile(h, i, q * PTILES + j)
                    a = a * a
                    rows[i][j % 4] = a if rows[i][j % 4] is None else rows[i][j % 4] + a
                    sums.append(a[:8] + a[8:])
                s[h, q, 8 * i : 8 * i + 8, :] = fold8(sums[:8])
                last.append(sums[8])
            s[h, q, 24:32, :] = fold8(last + [zero] * (8 - STEPS))

    sp_copies = [
        remote(s.at[0, pl.ds(m * 4, 4)], s_in.at[pl.ds(m * 4, 4)], sp_r.at[m], pair) for m in range(2)
    ]
    squares(0)

    @pl.when(k == 1)
    def _():
        pl.semaphore_wait(barrier, 1)
        signal(sem_p, [pair])

    @pl.when(k == 0)
    def _():
        pl.semaphore_wait(sem_p, 1)

    for copy in sp_copies:
        copy.start()
    squares(1)

    packed = jnp.zeros((LROWS, 128), F32)
    for i in range(STEPS):
        total = (rows[i][0] + rows[i][1]) + (rows[i][2] + rows[i][3])
        packed = jnp.where(lane == sublane + LROWS * i, jnp.sum(total, axis=1, keepdims=True), packed)
    rowbox[y] = jnp.sum(packed, axis=0, keepdims=True)

    @pl.when(k == 0)
    def _():
        pl.semaphore_wait(barrier, 18)
        signal(sem_p, [pair])

    @pl.when(k == 1)
    def _():
        pl.semaphore_wait(sem_p, 1)

    for d in ys:
        remote(rowbox.at[y], rowbox.at[y], box_r, d).start()

    def scatter_x(mine, ref, recv):
        ref[x] = mine[x]
        for n, d in enumerate(order):
            remote(mine.at[xx[d]], ref.at[x], recv, xs[n]).start()

    def scatter_z(mine, ref, recv):
        ref[4 + z] = mine[4 + z]
        for n, d in enumerate(order):
            remote(mine.at[4 + zz[d]], ref.at[4 + z], recv, zs[n]).start()

    def four(ref, first=0):
        return (ref[first] + ref[first + 1]) + (ref[first + 2] + ref[first + 3])

    sp_copies[0].wait_recv()
    for q in range(4):
        s_sum[q] = s[1, q] + s_in[q]
    scatter_x(s_sum, r1, r1_r)
    sp_copies[1].wait_recv()
    for q in range(4, 8):
        s_sum[q] = s[1, q] + s_in[q]
    scatter_z(s_sum, r1, r1_r)
    signal(sem_c, xs)

    def norm(h):
        def group(n, acc):
            for j in range(8):
                a = p[h, :, pl.ds(pl.multiple_of(n * 1024 + j * 128, 128), 128)]
                a = a * a
                acc = acc + (a[:8] + a[8:])
            return acc

        return group

    psum = zero
    pltpu.make_async_copy(loaded, loaded, load_sem).wait()
    for h in range(2):
        psum = lax.fori_loop(0, HCOLS // 1024, norm(h), psum)
    pl.semaphore_wait(sem_c, 3)
    signal(sem_d, zs)

    several(rowbox, 3, box_r).wait_recv()
    row_load.wait()
    totals = (rowbox[0] + rowbox[1]) + (rowbox[2] + rowbox[3])
    i0 = lax.broadcasted_iota(jnp.int32, (LROWS, LROWS), 0)
    i1 = lax.broadcasted_iota(jnp.int32, (LROWS, LROWS), 1)
    state = jnp.sum(jnp.where(i0 == i1, row_ref[...], 0.0), axis=1, keepdims=True)
    rr = []
    for i in range(STEPS):
        total = jnp.sum(jnp.where(lane == sublane + LROWS * i, totals, 0.0), axis=1, keepdims=True)
        state = rate[i][0] * state + rate[i][1] * (total / COLS)
        rr.append(jnp.broadcast_to(lax.rsqrt(state), (LROWS, 128)))
    newrow_ref[...] = jnp.sum(jnp.where(i0 == i1, state, 0.0), axis=0, keepdims=True)

    def products(h):
        def piece(q, _):
            sums = [[] for _ in range(PRODUCTS)]
            for j in range(PTILES):
                cols = pl.ds(pl.multiple_of(q * PCOLS + j * 128, 128), 128)
                a = [g[h, i, :, cols].astype(F32) * rr[i] for i in range(STEPS)]
                b = p[h, :, cols]
                for m, v in enumerate((a[0] * a[0], a[1] * a[1], a[2] * a[2], a[0] * a[1], a[0] * b, a[1] * b)):
                    sums[m].append(v[:8] + v[8:])
            for m in range(PRODUCTS):
                w[h, q, 8 * m : 8 * m + 8, :] = fold8(sums[m][:8])
            w[h, q, 48:56, :] = fold8([*[v[8] for v in sums], zero, zero])
            return 0

        return piece

    wp_copies = [
        remote(w.at[0, pl.ds(m * 4, 4)], w_in.at[pl.ds(m * 4, 4)], wp_r.at[m], pair) for m in range(2)
    ]
    for m in range(2):
        lax.fori_loop(m * 4, m * 4 + 4, products(0), 0)
        wp_copies[m].start()

    several(r1, 6, r1_r).wait_recv()
    r2[z] = four(r1)
    for d in zs:
        remote(r2.at[z], r2.at[z], r2_r, d).start()
    r2[4 + x] = four(r1, 4)
    for d in xs:
        remote(r2.at[4 + x], r2.at[4 + x], r2_r, d).start()

    lax.fori_loop(0, 4, products(1), 0)
    wp_copies[0].wait_recv()
    for q in range(4):
        w_sum[q] = w[1, q] + w_in[q]
    scatter_x(w_sum, wr, wr_r)
    lax.fori_loop(4, 8, products(1), 0)
    wp_copies[1].wait_recv()
    for q in range(4, 8):
        w_sum[q] = w[1, q] + w_in[q]
    scatter_z(w_sum, wr, wr_r)

    scale = []
    several(r2, 6, r2_r).wait_recv()
    for axis, mine in ((0, x), (1, z + 4)):
        sums = four(r2, 4 * axis)
        first = mine * PTILES
        state8, state1 = col_ref[pl.ds(first, 8), :], col_ref[pl.ds(first + 8, 1), :]
        scale8, scale1 = [], []
        for i in range(STEPS):
            state8 = rate[i][0] * state8 + rate[i][1] * (sums[8 * i : 8 * i + 8] / ROWS)
            state1 = rate[i][0] * state1 + rate[i][1] * (sums[24 + i : 25 + i] / ROWS)
            c[1, mine, 8 * i : 8 * i + 8, :] = state8
            c[1, mine, 24 + i : 25 + i, :] = state1
            scale8.append(lax.rsqrt(state8))
            scale1.append(lax.rsqrt(state1))
        scale.append((scale8, scale1))
        for d in zs if axis else xs:
            remote(c.at[1, mine], c.at[1, mine], c_r, d).start()

    acc = [None] * PRODUCTS
    extra = None
    several(wr, 6, wr_r).wait_recv()
    for axis in range(2):
        sums = four(wr, 4 * axis)
        q8, q1 = scale[axis]
        for m, f in enumerate((q8[0] * q8[0], q8[1] * q8[1], q8[2] * q8[2], q8[0] * q8[1], q8[0], q8[1])):
            v = f * sums[8 * m : 8 * m + 8]
            acc[m] = v if axis == 0 else acc[m] + v
        f = (q1[0] * q1[0], q1[1] * q1[1], q1[2] * q1[2], q1[0] * q1[1], q1[0], q1[1], q1[0] * 0.0, q1[0] * 0.0)
        v = jnp.concatenate(f, axis=0) * sums[48:56]
        extra = v if axis == 0 else extra + v
    sums = jnp.sum(fold8([*acc, psum, zero]) + extra, axis=1, keepdims=True)
    j0 = lax.broadcasted_iota(jnp.int32, (8, 128), 0)
    j1 = lax.broadcasted_iota(jnp.int32, (8, 128), 1)
    me = y * NROW + row
    bbox[me] = jnp.sum(jnp.where(j0 == j1, sums, 0.0), axis=0, keepdims=True)
    pl.semaphore_wait(sem_d, 3)
    for off in far_first():
        remote(bbox.at[me], bbox.at[me], b_r, at(*off)).start()

    def updates(h):
        def piece(q, _):
            scales = lax.rsqrt(c[h, q])
            for j in range(PTILES):
                cols = pl.ds(pl.multiple_of(q * PCOLS + j * 128, 128), 128)
                for i in range(STEPS):
                    at_row = 8 * i + j if j < 8 else 24 + i
                    u[h, i, :, cols] = g[h, i, :, cols].astype(F32) * rr[i] * scales[at_row : at_row + 1]
            return 0

        return piece

    c_copy = remote(c.at[1], c.at[0], cp_r, pair)
    several(c.at[1], 6, c_r).wait_recv()
    c_copy.start()
    for h in (1, 0):
        if h == 0:
            c_copy.wait_recv()
        lax.fori_loop(0, PIECES, updates(h), 0)
        for q in range(PIECES):
            newcol_ref[h, q * PTILES : q * PTILES + 8, :] = c[h, q, 16:24, :]
            newcol_ref[h, q * PTILES + 8 : q * PTILES + 9, :] = c[h, q, 26:27, :]

    several(bbox, NALL - 1, b_r).wait_recv()
    sums = jnp.sum(bbox[...], axis=0)
    j1 = lax.broadcasted_iota(jnp.int32, (1, 128), 1)
    uu0, uu1, uu2, u01, pu0, pu1, pp = [
        jnp.sum(jnp.where(j1 == m, sums, 0.0), axis=1, keepdims=True) for m in range(7)
    ]
    count = float(ROWS * COLS)
    clip = [jnp.maximum(1.0, jnp.sqrt(v / count)) for v in (uu0, uu1, uu2)]
    f0 = rate[0][2] * jnp.sqrt(pp / count) / clip[0]
    pp = pp - 2.0 * f0 * pu0 + f0 * f0 * uu0
    f1 = rate[1][2] * jnp.sqrt(pp / count) / clip[1]
    pp = pp - 2.0 * f1 * (pu1 - f0 * u01) + f1 * f1 * uu1
    f2 = rate[2][2] * jnp.sqrt(pp / count) / clip[2]
    for i, v in enumerate((f0, f1, f2)):
        factor_ref[i] = jnp.broadcast_to(v, (8, 128))

    remote(sent, sent, b_r, pair).wait_send()


def finish(p, u, factor_ref, newrow_ref, newcol_ref, out_hbm, row_hbm, col_hbm, o, written, out_sem, row_sem):
    k = lax.rem(lax.axis_index("row"), 2)
    halves = (1 - k, k)
    outs = [pltpu.make_async_copy(newrow_ref, row_hbm, row_sem)]
    for h in range(2):
        tiles = pl.ds(pl.multiple_of(halves[h] * HALF, 8), HALF)
        outs.append(pltpu.make_async_copy(newcol_ref.at[h], col_hbm.at[tiles], out_sem))
    for out in outs:
        out.start()
    f = [jnp.concatenate([factor_ref[i], factor_ref[i]], axis=0) for i in range(STEPS)]
    width = HCOLS // OUT_PARTS
    for h in range(2):
        for part in range(OUT_PARTS):
            for n in range(width // 128):
                cols = pl.ds(part * width + n * 128, 128)
                a = p[h, :, cols] - f[0] * u[h, 0, :, cols]
                o[h, :, cols] = a - (f[1] * u[h, 1, :, cols] + f[2] * u[h, 2, :, cols])
            src = o.at[h, :, pl.ds(part * width, width)]
            dst = out_hbm.at[:, pl.ds(pl.multiple_of(halves[h] * HCOLS + part * width, 128), width)]
            pltpu.make_async_copy(src, dst, out_sem).start()
    outs[0].wait()
    pltpu.make_async_copy(written, written, out_sem).wait()


def local(gradients, parameter, row_state, col_state):
    args = (gradients, parameter, row_state.reshape(1, LROWS), col_state.reshape(TILES, 128))
    vmem = pl.BlockSpec(memory_space=pltpu.VMEM)
    hbm = pl.BlockSpec(memory_space=pltpu.HBM)
    dma = pltpu.SemaphoreType.DMA
    regular, two = pltpu.SemaphoreType.REGULAR, dma((2,))
    state = pl.pallas_call(
        kernel,
        name="exchange",
        out_shape=(
            jax.ShapeDtypeStruct((2, LROWS, HCOLS), F32),
            jax.ShapeDtypeStruct((2, STEPS, LROWS, HCOLS), F32),
            jax.ShapeDtypeStruct((STEPS, 8, 128), F32),
            jax.ShapeDtypeStruct((1, LROWS), F32),
            jax.ShapeDtypeStruct((2, HALF, 128), F32),
        ),
        in_specs=[hbm] * 4,
        out_specs=(vmem,) * 5,
        scratch_shapes=[
            pltpu.VMEM((2, STEPS, LROWS, HCOLS), jnp.bfloat16),
            pltpu.VMEM((1, LROWS), F32),
            pltpu.VMEM((HALF, 128), F32),
            pltpu.VMEM((2, PIECES, SROWS, 128), F32),
            pltpu.VMEM((PIECES, SROWS, 128), F32),
            pltpu.VMEM((PIECES, SROWS, 128), F32),
            pltpu.VMEM((NX + NZ, SROWS, 128), F32),
            pltpu.VMEM((NZ + NX, SROWS, 128), F32),
            pltpu.VMEM((NY, 1, 128), F32),
            pltpu.VMEM((2, PIECES, WROWS, 128), F32),
            pltpu.VMEM((PIECES, WROWS, 128), F32),
            pltpu.VMEM((PIECES, WROWS, 128), F32),
            pltpu.VMEM((NX + NZ, WROWS, 128), F32),
            pltpu.VMEM((2, PIECES, SROWS, 128), F32),
            pltpu.VMEM((NALL, 1, 128), F32),
            pltpu.VMEM((LOADED, 1, 128), F32),
            pltpu.VMEM((SENT, 1, 128), F32),
            two, dma, dma, dma, two, dma, dma, dma, two, dma, dma, dma, dma, regular, regular, regular,
        ],
        compiler_params=pltpu.CompilerParams(
            collective_id=0, has_side_effects=True, vmem_limit_bytes=40 * 2**20
        ),
        cost_estimate=pl.CostEstimate(flops=20_000_000, bytes_accessed=4_200_000, transcendentals=100_000),
    )(*[pltpu.with_memory_space_constraint(a, pltpu.HBM) for a in args])
    new_param, new_row, new_col = pl.pallas_call(
        finish,
        name="finish",
        out_shape=(
            jax.ShapeDtypeStruct((LROWS, LCOLS), F32),
            jax.ShapeDtypeStruct((1, LROWS), F32),
            jax.ShapeDtypeStruct((TILES, 128), F32),
        ),
        in_specs=[vmem] * 5,
        out_specs=(hbm,) * 3,
        scratch_shapes=[
            pltpu.VMEM((2, LROWS, HCOLS), F32),
            pltpu.VMEM((LROWS * TILES + TILES, 1, 128), F32),
            dma, dma,
        ],
        compiler_params=pltpu.CompilerParams(vmem_limit_bytes=40 * 2**20),
        cost_estimate=pl.CostEstimate(flops=2_000_000, bytes_accessed=1_200_000, transcendentals=0),
    )(*state)
    return new_param, new_row.reshape(LROWS), new_col.reshape(LCOLS)


def solution(mesh):
    placed = (P(None, "row", "col"), P("row", "col"), P("row"), P("col"))
    return jax.shard_map(
        local,
        mesh=mesh,
        in_specs=placed,
        out_specs=(P("row", "col"), P("row"), P("col")),
        check_vma=False,
    )
```

```python
import functools

import jax
import jax.numpy as jnp
import numpy as np
from jax import lax
from jax.experimental import pallas as pl
from jax.experimental.pallas import tpu as pltpu
from jax.sharding import PartitionSpec as P

MESH = pl.DeviceIdType.MESH
START = 100
F32 = jnp.float32

NZ, NX, NK, NY = 4, 4, 2, 4
NROW, NALL = NZ * NX * NK, NZ * NX * NK * NY
STEPS, LROWS, LCOLS = 3, 16, 18432
ROWS, COLS = LROWS * NROW, LCOLS * NY
TILES = LCOLS // 128
HALF, HCOLS = TILES // 2, LCOLS // 2
PIECES = 8
PTILES = HALF // PIECES
PCOLS = PTILES * 128
SROWS = 32
WROWS = 56
PRODUCTS = 6
SENT = 2 * PIECES * SROWS + PIECES * WROWS + 6 * (3 * SROWS + WROWS) + NY - 1 + NALL - 1
LOADED = LROWS * TILES + HALF
OUT_PARTS = 3


def far_first():
    dist = (0, 1, 2, 1)
    offs = [(dz, dx, dy, dk) for dz in range(NZ) for dx in range(NX) for dy in range(NY) for dk in range(NK)]
    offs = [o for o in offs if o != (0, 0, 0, 0)]
    return sorted(offs, key=lambda o: (-(dist[o[0]] + dist[o[1]] + dist[o[2]]), -o[3]))


def rates():
    out = []
    for k in range(STEPS):
        t = np.float32(START + 1 + k)
        forget = np.float32(1.0) - np.power(t, np.float32(-0.8))
        out.append((float(forget), float(np.float32(1.0) - forget), float(np.power(t, np.float32(-0.5)))))
    return out


def up(x, n):
    return pltpu.roll(x, 8 - n, 0)


def down(x, n):
    return pltpu.roll(x, n, 0)


def fold8(v):
    s = lax.broadcasted_iota(jnp.int32, (8, 128), 0)
    m4, m2, m1 = s < 4, lax.rem(s, 4) < 2, lax.rem(s, 2) < 1
    w = [jnp.where(m4, v[i], v[i + 4]) + up(jnp.where(m4, v[i + 4], v[i]), 4) for i in range(4)]
    x = [jnp.where(m2, w[i] + up(w[i], 2), w[i + 2] + down(w[i + 2], 2)) for i in range(2)]
    return jnp.where(m1, x[0] + up(x[0], 1), x[1] + down(x[1], 1))


def kernel(
    grad_hbm, param_hbm, row_hbm, col_hbm,
    p, u, factor_ref, newrow_ref, newcol_ref,
    g, row_ref, col_ref, s, s_in, s_sum, r1, r2, rowbox, w, w_in, w_sum, wr, c, bbox, loaded, sent,
    g_sem, row_sem, load_sem, send, sp_r, r1_r, r2_r, box_r, wp_r, wr_r, c_r, cp_r, b_r, sem_p, sem_c, sem_d,
):
    rate = rates()
    row, y = lax.axis_index("row"), lax.axis_index("col")
    z, x, k = lax.div(row, 8), lax.rem(lax.div(row, 2), 4), lax.rem(row, 2)
    zz = [z, *[lax.rem(z + d, NZ) for d in range(1, NZ)]]
    xx = [x, *[lax.rem(x + d, NX) for d in range(1, NX)]]
    yy = [y, *[lax.rem(y + d, NY) for d in range(1, NY)]]
    kk = [k, 1 - k]

    def at(dz=0, dx=0, dy=0, dk=0):
        return (zz[dz] * 8 + xx[dx] * 2 + kk[dk], yy[dy])

    order = (2, 1, 3)
    pair = at(dk=1)
    xs = [at(dx=d) for d in order]
    zs = [at(dz=d) for d in order]
    ys = [at(dy=d) for d in order]

    def signal(sem, devices):
        for d in devices:
            pl.semaphore_signal(sem, inc=1, device_id=d, device_id_type=MESH)

    def remote(src, dst, recv, device):
        return pltpu.make_async_remote_copy(src, dst, send, recv, device_id=device, device_id_type=MESH)

    def several(ref, count, recv):
        return remote(ref.at[pl.ds(0, count)], ref.at[pl.ds(0, count)], recv, pair)

    halves = (1 - k, k)

    def columns(h):
        return pl.ds(pl.multiple_of(halves[h] * HCOLS, 128), HCOLS)

    barrier = pltpu.get_barrier_semaphore()
    g_loads = [pltpu.make_async_copy(grad_hbm.at[:, :, columns(h)], g.at[h], g_sem.at[h]) for h in range(2)]
    p_loads = [pltpu.make_async_copy(param_hbm.at[:, columns(h)], p.at[h], load_sem) for h in range(2)]
    col_load = pltpu.make_async_copy(col_hbm.at[pl.ds(pl.multiple_of(k * HALF, 8), HALF)], col_ref, load_sem)
    row_load = pltpu.make_async_copy(row_hbm, row_ref, row_sem)
    g_loads[0].start()
    signal(barrier, [(d[0] - k, d[1]) for d in (*zs, *xs, *ys)])

    @pl.when(k == 0)
    def _():
        signal(barrier, [pair])

    for load in (g_loads[1], row_load, col_load, *p_loads):
        load.start()

    lane = lax.broadcasted_iota(jnp.int32, (LROWS, 128), 1)
    sublane = lax.broadcasted_iota(jnp.int32, (LROWS, 128), 0)
    zero = jnp.zeros((8, 128), F32)

    def tile(h, i, n):
        return g[h, i, :, n * 128 : (n + 1) * 128].astype(F32)

    rows = [[None] * 4 for _ in range(STEPS)]

    def squares(h):
        g_loads[h].wait()
        for q in range(PIECES):
            last = []
            for i in range(STEPS):
                sums = []
                for j in range(PTILES):
                    a = tile(h, i, q * PTILES + j)
                    a = a * a
                    rows[i][j % 4] = a if rows[i][j % 4] is None else rows[i][j % 4] + a
                    sums.append(a[:8] + a[8:])
                s[h, q, 8 * i : 8 * i + 8, :] = fold8(sums[:8])
                last.append(sums[8])
            s[h, q, 24:32, :] = fold8(last + [zero] * (8 - STEPS))

    sp_copies = [
        remote(s.at[0, pl.ds(m * 4, 4)], s_in.at[pl.ds(m * 4, 4)], sp_r.at[m], pair) for m in range(2)
    ]
    squares(0)

    @pl.when(k == 1)
    def _():
        pl.semaphore_wait(barrier, 1)
        signal(sem_p, [pair])

    @pl.when(k == 0)
    def _():
        pl.semaphore_wait(sem_p, 1)

    for copy in sp_copies:
        copy.start()
    squares(1)

    packed = jnp.zeros((LROWS, 128), F32)
    for i in range(STEPS):
        total = (rows[i][0] + rows[i][1]) + (rows[i][2] + rows[i][3])
        packed = jnp.where(lane == sublane + LROWS * i, jnp.sum(total, axis=1, keepdims=True), packed)
    rowbox[y] = jnp.sum(packed, axis=0, keepdims=True)

    @pl.when(k == 0)
    def _():
        pl.semaphore_wait(barrier, 18)
        signal(sem_p, [pair])

    @pl.when(k == 1)
    def _():
        pl.semaphore_wait(sem_p, 1)

    for d in ys:
        remote(rowbox.at[y], rowbox.at[y], box_r, d).start()

    def scatter_x(mine, ref, recv):
        ref[x] = mine[x]
        for n, d in enumerate(order):
            remote(mine.at[xx[d]], ref.at[x], recv, xs[n]).start()

    def scatter_z(mine, ref, recv):
        ref[4 + z] = mine[4 + z]
        for n, d in enumerate(order):
            remote(mine.at[4 + zz[d]], ref.at[4 + z], recv, zs[n]).start()

    def four(ref, first=0):
        return (ref[first] + ref[first + 1]) + (ref[first + 2] + ref[first + 3])

    sp_copies[0].wait_recv()
    for q in range(4):
        s_sum[q] = s[1, q] + s_in[q]
    scatter_x(s_sum, r1, r1_r)
    sp_copies[1].wait_recv()
    for q in range(4, 8):
        s_sum[q] = s[1, q] + s_in[q]
    scatter_z(s_sum, r1, r1_r)
    signal(sem_c, xs)

    def norm(h):
        def group(n, acc):
            for j in range(8):
                a = p[h, :, pl.ds(pl.multiple_of(n * 1024 + j * 128, 128), 128)]
                a = a * a
                acc = acc + (a[:8] + a[8:])
            return acc

        return group

    psum = zero
    pltpu.make_async_copy(loaded, loaded, load_sem).wait()
    for h in range(2):
        psum = lax.fori_loop(0, HCOLS // 1024, norm(h), psum)
    pl.semaphore_wait(sem_c, 3)
    signal(sem_d, zs)

    row_load.wait()
    i0 = lax.broadcasted_iota(jnp.int32, (LROWS, LROWS), 0)
    i1 = lax.broadcasted_iota(jnp.int32, (LROWS, LROWS), 1)
    state = jnp.sum(jnp.where(i0 == i1, row_ref[...], 0.0), axis=1, keepdims=True)
    several(rowbox, 3, box_r).wait_recv()
    totals = (rowbox[0] + rowbox[1]) + (rowbox[2] + rowbox[3])
    rr = []
    for i in range(STEPS):
        total = jnp.sum(jnp.where(lane == sublane + LROWS * i, totals, 0.0), axis=1, keepdims=True)
        state = rate[i][0] * state + rate[i][1] * (total / COLS)
        rr.append(jnp.broadcast_to(lax.rsqrt(state), (LROWS, 128)))

    def products(h):
        def piece(q, _):
            sums = [[] for _ in range(PRODUCTS)]
            for j in range(PTILES):
                cols = pl.ds(pl.multiple_of(q * PCOLS + j * 128, 128), 128)
                a = [g[h, i, :, cols].astype(F32) * rr[i] for i in range(STEPS)]
                b = p[h, :, cols]
                for m, v in enumerate((a[0] * a[0], a[1] * a[1], a[2] * a[2], a[0] * a[1], a[0] * b, a[1] * b)):
                    sums[m].append(v[:8] + v[8:])
            for m in range(PRODUCTS):
                w[h, q, 8 * m : 8 * m + 8, :] = fold8(sums[m][:8])
            w[h, q, 48:56, :] = fold8([*[v[8] for v in sums], zero, zero])
            if h == 0:
                remote(w.at[0, q], w_in.at[q], wp_r.at[lax.div(q, 4)], pair).start()
            return 0

        return piece

    wp_copies = [
        remote(w.at[0, pl.ds(m * 4, 4)], w_in.at[pl.ds(m * 4, 4)], wp_r.at[m], pair) for m in range(2)
    ]
    lax.fori_loop(0, PIECES, products(0), 0)

    several(r1, 6, r1_r).wait_recv()
    r2[z] = four(r1)
    for d in zs:
        remote(r2.at[z], r2.at[z], r2_r, d).start()
    r2[4 + x] = four(r1, 4)
    for d in xs:
        remote(r2.at[4 + x], r2.at[4 + x], r2_r, d).start()

    lax.fori_loop(0, 4, products(1), 0)
    wp_copies[0].wait_recv()
    for q in range(4):
        w_sum[q] = w[1, q] + w_in[q]
    scatter_x(w_sum, wr, wr_r)
    lax.fori_loop(4, 8, products(1), 0)
    wp_copies[1].wait_recv()
    for q in range(4, 8):
        w_sum[q] = w[1, q] + w_in[q]
    scatter_z(w_sum, wr, wr_r)

    scale = []
    several(r2, 6, r2_r).wait_recv()
    for axis, mine in ((0, x), (1, z + 4)):
        sums = four(r2, 4 * axis)
        first = mine * PTILES
        state8, state1 = col_ref[pl.ds(first, 8), :], col_ref[pl.ds(first + 8, 1), :]
        scale8, scale1 = [], []
        for i in range(STEPS):
            state8 = rate[i][0] * state8 + rate[i][1] * (sums[8 * i : 8 * i + 8] / ROWS)
            state1 = rate[i][0] * state1 + rate[i][1] * (sums[24 + i : 25 + i] / ROWS)
            c[1, mine, 8 * i : 8 * i + 8, :] = state8
            c[1, mine, 24 + i : 25 + i, :] = state1
            scale8.append(lax.rsqrt(state8))
            scale1.append(lax.rsqrt(state1))
        scale.append((scale8, scale1))
        for d in zs if axis else xs:
            remote(c.at[1, mine], c.at[1, mine], c_r, d).start()

    acc = [None] * PRODUCTS
    extra = None
    several(wr, 6, wr_r).wait_recv()
    for axis in range(2):
        sums = four(wr, 4 * axis)
        q8, q1 = scale[axis]
        for m, f in enumerate((q8[0] * q8[0], q8[1] * q8[1], q8[2] * q8[2], q8[0] * q8[1], q8[0], q8[1])):
            v = f * sums[8 * m : 8 * m + 8]
            acc[m] = v if axis == 0 else acc[m] + v
        f = (q1[0] * q1[0], q1[1] * q1[1], q1[2] * q1[2], q1[0] * q1[1], q1[0], q1[1], q1[0] * 0.0, q1[0] * 0.0)
        v = jnp.concatenate(f, axis=0) * sums[48:56]
        extra = v if axis == 0 else extra + v
    sums = jnp.sum(fold8([*acc, psum, zero]) + extra, axis=1, keepdims=True)
    j0 = lax.broadcasted_iota(jnp.int32, (8, 128), 0)
    j1 = lax.broadcasted_iota(jnp.int32, (8, 128), 1)
    me = y * NROW + row
    bbox[me] = jnp.sum(jnp.where(j0 == j1, sums, 0.0), axis=0, keepdims=True)
    pl.semaphore_wait(sem_d, 3)
    for off in far_first():
        remote(bbox.at[me], bbox.at[me], b_r, at(*off)).start()

    newrow_ref[...] = jnp.sum(jnp.where(i0 == i1, state, 0.0), axis=0, keepdims=True)

    def updates(h):
        def piece(q, _):
            scales = lax.rsqrt(c[h, q])
            for j in range(PTILES):
                cols = pl.ds(pl.multiple_of(q * PCOLS + j * 128, 128), 128)
                for i in range(STEPS):
                    at_row = 8 * i + j if j < 8 else 24 + i
                    u[h, i, :, cols] = g[h, i, :, cols].astype(F32) * rr[i] * scales[at_row : at_row + 1]
            return 0

        return piece

    c_copy = remote(c.at[1], c.at[0], cp_r, pair)
    several(c.at[1], 6, c_r).wait_recv()
    c_copy.start()
    for h in (1, 0):
        if h == 0:
            c_copy.wait_recv()
        lax.fori_loop(0, PIECES, updates(h), 0)
        for q in range(PIECES):
            newcol_ref[h, q * PTILES : q * PTILES + 8, :] = c[h, q, 16:24, :]
            newcol_ref[h, q * PTILES + 8 : q * PTILES + 9, :] = c[h, q, 26:27, :]

    several(bbox, NALL - 1, b_r).wait_recv()
    sums = [bbox[i] for i in range(NALL)]
    while len(sums) > 1:
        sums = [sums[i] + sums[i + 1] for i in range(0, len(sums), 2)]
    sums = sums[0]
    j1 = lax.broadcasted_iota(jnp.int32, (1, 128), 1)
    uu0, uu1, uu2, u01, pu0, pu1, pp = [
        jnp.sum(jnp.where(j1 == m, sums, 0.0), axis=1, keepdims=True) for m in range(7)
    ]
    count = float(ROWS * COLS)
    clip = [jnp.minimum(1.0, lax.rsqrt(v * (1.0 / count))) for v in (uu0, uu1, uu2)]
    f0 = rate[0][2] * clip[0] * jnp.sqrt(pp * (1.0 / count))
    pp = pp - 2.0 * f0 * pu0 + f0 * f0 * uu0
    f1 = rate[1][2] * clip[1] * jnp.sqrt(pp * (1.0 / count))
    pp = pp - 2.0 * f1 * (pu1 - f0 * u01) + f1 * f1 * uu1
    f2 = rate[2][2] * clip[2] * jnp.sqrt(pp * (1.0 / count))
    for i, v in enumerate((f0, f1, f2)):
        factor_ref[i] = jnp.broadcast_to(v, (8, 128))

    remote(sent, sent, b_r, pair).wait_send()


def finish(p, u, factor_ref, newrow_ref, newcol_ref, out_hbm, row_hbm, col_hbm, o, written, out_sem, row_sem):
    k = lax.rem(lax.axis_index("row"), 2)
    halves = (1 - k, k)
    outs = [pltpu.make_async_copy(newrow_ref, row_hbm, row_sem)]
    for h in range(2):
        tiles = pl.ds(pl.multiple_of(halves[h] * HALF, 8), HALF)
        outs.append(pltpu.make_async_copy(newcol_ref.at[h], col_hbm.at[tiles], out_sem))
    for out in outs:
        out.start()
    f = [jnp.concatenate([factor_ref[i], factor_ref[i]], axis=0) for i in range(STEPS)]
    width = HCOLS // OUT_PARTS
    for h in range(2):
        for part in range(OUT_PARTS):
            for n in range(width // 128):
                cols = pl.ds(part * width + n * 128, 128)
                a = p[h, :, cols] - f[0] * u[h, 0, :, cols]
                o[h, :, cols] = a - (f[1] * u[h, 1, :, cols] + f[2] * u[h, 2, :, cols])
            src = o.at[h, :, pl.ds(part * width, width)]
            dst = out_hbm.at[:, pl.ds(pl.multiple_of(halves[h] * HCOLS + part * width, 128), width)]
            pltpu.make_async_copy(src, dst, out_sem).start()
    outs[0].wait()
    pltpu.make_async_copy(written, written, out_sem).wait()


def local(gradients, parameter, row_state, col_state):
    args = (gradients, parameter, row_state.reshape(1, LROWS), col_state.reshape(TILES, 128))
    vmem = pl.BlockSpec(memory_space=pltpu.VMEM)
    hbm = pl.BlockSpec(memory_space=pltpu.HBM)
    dma = pltpu.SemaphoreType.DMA
    regular, two = pltpu.SemaphoreType.REGULAR, dma((2,))
    state = pl.pallas_call(
        kernel,
        name="exchange",
        out_shape=(
            jax.ShapeDtypeStruct((2, LROWS, HCOLS), F32),
            jax.ShapeDtypeStruct((2, STEPS, LROWS, HCOLS), F32),
            jax.ShapeDtypeStruct((STEPS, 8, 128), F32),
            jax.ShapeDtypeStruct((1, LROWS), F32),
            jax.ShapeDtypeStruct((2, HALF, 128), F32),
        ),
        in_specs=[hbm] * 4,
        out_specs=(vmem,) * 5,
        scratch_shapes=[
            pltpu.VMEM((2, STEPS, LROWS, HCOLS), jnp.bfloat16),
            pltpu.VMEM((1, LROWS), F32),
            pltpu.VMEM((HALF, 128), F32),
            pltpu.VMEM((2, PIECES, SROWS, 128), F32),
            pltpu.VMEM((PIECES, SROWS, 128), F32),
            pltpu.VMEM((PIECES, SROWS, 128), F32),
            pltpu.VMEM((NX + NZ, SROWS, 128), F32),
            pltpu.VMEM((NZ + NX, SROWS, 128), F32),
            pltpu.VMEM((NY, 1, 128), F32),
            pltpu.VMEM((2, PIECES, WROWS, 128), F32),
            pltpu.VMEM((PIECES, WROWS, 128), F32),
            pltpu.VMEM((PIECES, WROWS, 128), F32),
            pltpu.VMEM((NX + NZ, WROWS, 128), F32),
            pltpu.VMEM((2, PIECES, SROWS, 128), F32),
            pltpu.VMEM((NALL, 1, 128), F32),
            pltpu.VMEM((LOADED, 1, 128), F32),
            pltpu.VMEM((SENT, 1, 128), F32),
            two, dma, dma, dma, two, dma, dma, dma, two, dma, dma, dma, dma, regular, regular, regular,
        ],
        compiler_params=pltpu.CompilerParams(
            collective_id=0, has_side_effects=True, vmem_limit_bytes=40 * 2**20
        ),
        cost_estimate=pl.CostEstimate(flops=20_000_000, bytes_accessed=4_200_000, transcendentals=100_000),
    )(*[pltpu.with_memory_space_constraint(a, pltpu.HBM) for a in args])
    new_param, new_row, new_col = pl.pallas_call(
        finish,
        name="finish",
        out_shape=(
            jax.ShapeDtypeStruct((LROWS, LCOLS), F32),
            jax.ShapeDtypeStruct((1, LROWS), F32),
            jax.ShapeDtypeStruct((TILES, 128), F32),
        ),
        in_specs=[vmem] * 5,
        out_specs=(hbm,) * 3,
        scratch_shapes=[
            pltpu.VMEM((2, LROWS, HCOLS), F32),
            pltpu.VMEM((LROWS * TILES + TILES, 1, 128), F32),
            dma, dma,
        ],
        compiler_params=pltpu.CompilerParams(vmem_limit_bytes=40 * 2**20),
        cost_estimate=pl.CostEstimate(flops=2_000_000, bytes_accessed=1_200_000, transcendentals=0),
    )(*state)
    return new_param, new_row.reshape(LROWS), new_col.reshape(LCOLS)


def solution(mesh):
    placed = (P(None, "row", "col"), P("row", "col"), P("row"), P("col"))
    return jax.shard_map(
        local,
        mesh=mesh,
        in_specs=placed,
        out_specs=(P("row", "col"), P("row"), P("col")),
        check_vma=False,
    )
```

```python
import functools

import jax
import jax.numpy as jnp
import numpy as np
from jax import lax
from jax.experimental import pallas as pl
from jax.experimental.pallas import tpu as pltpu
from jax.sharding import PartitionSpec as P

MESH = pl.DeviceIdType.MESH
START = 100
F32 = jnp.float32

NZ, NX, NK, NY = 4, 4, 2, 4
NROW, NALL = NZ * NX * NK, NZ * NX * NK * NY
STEPS, LROWS, LCOLS = 3, 16, 18432
ROWS, COLS = LROWS * NROW, LCOLS * NY
TILES = LCOLS // 128
HALF, HCOLS = TILES // 2, LCOLS // 2
PIECES = 8
PTILES = HALF // PIECES
PCOLS = PTILES * 128
SROWS = 32
WROWS = 56
PRODUCTS = 6
SENT = 2 * PIECES * SROWS + PIECES * WROWS + 6 * (3 * SROWS + WROWS) + NY - 1 + NALL - 1
LOADED = LROWS * TILES + HALF
OUT_PARTS = 3


def far_first():
    dist = (0, 1, 2, 1)
    offs = [(dz, dx, dy, dk) for dz in range(NZ) for dx in range(NX) for dy in range(NY) for dk in range(NK)]
    offs = [o for o in offs if o != (0, 0, 0, 0)]
    return sorted(offs, key=lambda o: (-(dist[o[0]] + dist[o[1]] + dist[o[2]]), -o[3]))


def rates():
    out = []
    for k in range(STEPS):
        t = np.float32(START + 1 + k)
        forget = np.float32(1.0) - np.power(t, np.float32(-0.8))
        out.append((float(forget), float(np.float32(1.0) - forget), float(np.power(t, np.float32(-0.5)))))
    return out


def up(x, n):
    return pltpu.roll(x, 8 - n, 0)


def down(x, n):
    return pltpu.roll(x, n, 0)


def fold8(v):
    s = lax.broadcasted_iota(jnp.int32, (8, 128), 0)
    m4, m2, m1 = s < 4, lax.rem(s, 4) < 2, lax.rem(s, 2) < 1
    w = [jnp.where(m4, v[i], v[i + 4]) + up(jnp.where(m4, v[i + 4], v[i]), 4) for i in range(4)]
    x = [jnp.where(m2, w[i] + up(w[i], 2), w[i + 2] + down(w[i + 2], 2)) for i in range(2)]
    return jnp.where(m1, x[0] + up(x[0], 1), x[1] + down(x[1], 1))


def kernel(
    grad_hbm, param_hbm, row_hbm, col_hbm,
    p, u, factor_ref, newrow_ref, newcol_ref,
    g, row_ref, col_ref, s, s_in, s_sum, r1, r2, rowbox, w, w_in, w_sum, wr, c, bbox, loaded, sent,
    g_sem, row_sem, load_sem, send, sp_r, r1_r, r2_r, box_r, wp_r, wr_r, c_r, cp_r, b_r, sem_p, sem_c, sem_d,
):
    rate = rates()
    row, y = lax.axis_index("row"), lax.axis_index("col")
    z, x, k = lax.div(row, 8), lax.rem(lax.div(row, 2), 4), lax.rem(row, 2)
    zz = [z, *[lax.rem(z + d, NZ) for d in range(1, NZ)]]
    xx = [x, *[lax.rem(x + d, NX) for d in range(1, NX)]]
    yy = [y, *[lax.rem(y + d, NY) for d in range(1, NY)]]
    kk = [k, 1 - k]

    def at(dz=0, dx=0, dy=0, dk=0):
        return (zz[dz] * 8 + xx[dx] * 2 + kk[dk], yy[dy])

    order = (2, 1, 3)
    pair = at(dk=1)
    xs = [at(dx=d) for d in order]
    zs = [at(dz=d) for d in order]
    ys = [at(dy=d) for d in order]

    def signal(sem, devices):
        for d in devices:
            pl.semaphore_signal(sem, inc=1, device_id=d, device_id_type=MESH)

    def remote(src, dst, recv, device):
        return pltpu.make_async_remote_copy(src, dst, send, recv, device_id=device, device_id_type=MESH)

    def several(ref, count, recv):
        return remote(ref.at[pl.ds(0, count)], ref.at[pl.ds(0, count)], recv, pair)

    halves = (1 - k, k)

    def columns(h):
        return pl.ds(pl.multiple_of(halves[h] * HCOLS, 128), HCOLS)

    barrier = pltpu.get_barrier_semaphore()
    g_loads = [pltpu.make_async_copy(grad_hbm.at[:, :, columns(h)], g.at[h], g_sem.at[h]) for h in range(2)]
    p_loads = [pltpu.make_async_copy(param_hbm.at[:, columns(h)], p.at[h], load_sem) for h in range(2)]
    col_load = pltpu.make_async_copy(col_hbm.at[pl.ds(pl.multiple_of(k * HALF, 8), HALF)], col_ref, load_sem)
    row_load = pltpu.make_async_copy(row_hbm, row_ref, row_sem)
    g_loads[0].start()
    signal(barrier, [(d[0] - k, d[1]) for d in (*zs, *xs, *ys)])

    @pl.when(k == 0)
    def _():
        signal(barrier, [pair])

    for load in (g_loads[1], row_load, col_load, *p_loads):
        load.start()

    lane = lax.broadcasted_iota(jnp.int32, (LROWS, 128), 1)
    sublane = lax.broadcasted_iota(jnp.int32, (LROWS, 128), 0)
    zero = jnp.zeros((8, 128), F32)

    def tile(h, i, n):
        return g[h, i, :, n * 128 : (n + 1) * 128].astype(F32)

    rows = [[None] * 4 for _ in range(STEPS)]

    def squares(h):
        g_loads[h].wait()
        for q in range(PIECES):
            last = []
            for i in range(STEPS):
                sums = []
                for j in range(PTILES):
                    a = tile(h, i, q * PTILES + j)
                    a = a * a
                    rows[i][j % 4] = a if rows[i][j % 4] is None else rows[i][j % 4] + a
                    sums.append(a[:8] + a[8:])
                s[h, q, 8 * i : 8 * i + 8, :] = fold8(sums[:8])
                last.append(sums[8])
            s[h, q, 24:32, :] = fold8(last + [zero] * (8 - STEPS))

    sp_copies = [
        remote(s.at[0, pl.ds(m * 4, 4)], s_in.at[pl.ds(m * 4, 4)], sp_r.at[m], pair) for m in range(2)
    ]
    squares(0)

    @pl.when(k == 1)
    def _():
        pl.semaphore_wait(barrier, 1)
        signal(sem_p, [pair])

    @pl.when(k == 0)
    def _():
        pl.semaphore_wait(sem_p, 1)

    for copy in sp_copies:
        copy.start()
    squares(1)

    packed = jnp.zeros((LROWS, 128), F32)
    for i in range(STEPS):
        total = (rows[i][0] + rows[i][1]) + (rows[i][2] + rows[i][3])
        packed = jnp.where(lane == sublane + LROWS * i, jnp.sum(total, axis=1, keepdims=True), packed)
    rowbox[y] = jnp.sum(packed, axis=0, keepdims=True)

    @pl.when(k == 0)
    def _():
        pl.semaphore_wait(barrier, 18)
        signal(sem_p, [pair])

    @pl.when(k == 1)
    def _():
        pl.semaphore_wait(sem_p, 1)

    for d in ys:
        remote(rowbox.at[y], rowbox.at[y], box_r, d).start()

    def scatter_x(mine, ref, recv):
        ref[x] = mine[x]
        for n, d in enumerate(order):
            remote(mine.at[xx[d]], ref.at[x], recv, xs[n]).start()

    def scatter_z(mine, ref, recv):
        ref[4 + z] = mine[4 + z]
        for n, d in enumerate(order):
            remote(mine.at[4 + zz[d]], ref.at[4 + z], recv, zs[n]).start()

    def four(ref, first=0):
        return (ref[first] + ref[first + 1]) + (ref[first + 2] + ref[first + 3])

    sp_copies[0].wait_recv()
    for q in range(4):
        s_sum[q] = s[1, q] + s_in[q]
    scatter_x(s_sum, r1, r1_r.at[0])
    sp_copies[1].wait_recv()
    for q in range(4, 8):
        s_sum[q] = s[1, q] + s_in[q]
    scatter_z(s_sum, r1, r1_r.at[1])
    signal(sem_c, xs)

    def norm(h):
        def group(n, acc):
            for j in range(8):
                a = p[h, :, pl.ds(pl.multiple_of(n * 1024 + j * 128, 128), 128)]
                a = a * a
                acc = acc + (a[:8] + a[8:])
            return acc

        return group

    psum = zero
    pltpu.make_async_copy(loaded, loaded, load_sem).wait()
    for h in range(2):
        psum = lax.fori_loop(0, HCOLS // 1024, norm(h), psum)
    pl.semaphore_wait(sem_c, 3)
    signal(sem_d, zs)

    row_load.wait()
    i0 = lax.broadcasted_iota(jnp.int32, (LROWS, LROWS), 0)
    i1 = lax.broadcasted_iota(jnp.int32, (LROWS, LROWS), 1)
    state = jnp.sum(jnp.where(i0 == i1, row_ref[...], 0.0), axis=1, keepdims=True)
    several(rowbox, 3, box_r).wait_recv()
    totals = (rowbox[0] + rowbox[1]) + (rowbox[2] + rowbox[3])
    rr = []
    for i in range(STEPS):
        total = jnp.sum(jnp.where(lane == sublane + LROWS * i, totals, 0.0), axis=1, keepdims=True)
        state = rate[i][0] * state + rate[i][1] * (total / COLS)
        rr.append(jnp.broadcast_to(lax.rsqrt(state), (LROWS, 128)))

    def products(h):
        def piece(q, _):
            sums = [[] for _ in range(PRODUCTS)]
            for j in range(PTILES):
                cols = pl.ds(pl.multiple_of(q * PCOLS + j * 128, 128), 128)
                a = [g[h, i, :, cols].astype(F32) * rr[i] for i in range(STEPS)]
                b = p[h, :, cols]
                for m, v in enumerate((a[0] * a[0], a[1] * a[1], a[2] * a[2], a[0] * a[1], a[0] * b, a[1] * b)):
                    sums[m].append(v[:8] + v[8:])
            for m in range(PRODUCTS):
                w[h, q, 8 * m : 8 * m + 8, :] = fold8(sums[m][:8])
            w[h, q, 48:56, :] = fold8([*[v[8] for v in sums], zero, zero])
            if h == 0:
                remote(w.at[0, q], w_in.at[q], wp_r.at[lax.div(q, 4)], pair).start()
            return 0

        return piece

    wp_copies = [
        remote(w.at[0, pl.ds(m * 4, 4)], w_in.at[pl.ds(m * 4, 4)], wp_r.at[m], pair) for m in range(2)
    ]
    lax.fori_loop(0, PIECES, products(0), 0)

    several(r1, 3, r1_r.at[0]).wait_recv()
    r2[z] = four(r1)
    for d in zs:
        remote(r2.at[z], r2.at[z], r2_r, d).start()
    several(r1, 3, r1_r.at[1]).wait_recv()
    r2[4 + x] = four(r1, 4)
    for d in xs:
        remote(r2.at[4 + x], r2.at[4 + x], r2_r, d).start()

    lax.fori_loop(0, 4, products(1), 0)
    wp_copies[0].wait_recv()
    for q in range(4):
        w_sum[q] = w[1, q] + w_in[q]
    scatter_x(w_sum, wr, wr_r.at[0])
    lax.fori_loop(4, 8, products(1), 0)
    wp_copies[1].wait_recv()
    for q in range(4, 8):
        w_sum[q] = w[1, q] + w_in[q]
    scatter_z(w_sum, wr, wr_r.at[1])

    scale = []
    several(r2, 6, r2_r).wait_recv()
    for axis, mine in ((0, x), (1, z + 4)):
        sums = four(r2, 4 * axis)
        first = mine * PTILES
        state8, state1 = col_ref[pl.ds(first, 8), :], col_ref[pl.ds(first + 8, 1), :]
        scale8, scale1 = [], []
        for i in range(STEPS):
            state8 = rate[i][0] * state8 + rate[i][1] * (sums[8 * i : 8 * i + 8] / ROWS)
            state1 = rate[i][0] * state1 + rate[i][1] * (sums[24 + i : 25 + i] / ROWS)
            c[1, mine, 8 * i : 8 * i + 8, :] = state8
            c[1, mine, 24 + i : 25 + i, :] = state1
            scale8.append(lax.rsqrt(state8))
            scale1.append(lax.rsqrt(state1))
        scale.append((scale8, scale1))
        for d in zs if axis else xs:
            remote(c.at[1, mine], c.at[1, mine], c_r, d).start()

    acc = [None] * PRODUCTS
    extra = None
    for axis in range(2):
        several(wr, 3, wr_r.at[axis]).wait_recv()
        sums = four(wr, 4 * axis)
        q8, q1 = scale[axis]
        for m, f in enumerate((q8[0] * q8[0], q8[1] * q8[1], q8[2] * q8[2], q8[0] * q8[1], q8[0], q8[1])):
            v = f * sums[8 * m : 8 * m + 8]
            acc[m] = v if axis == 0 else acc[m] + v
        f = (q1[0] * q1[0], q1[1] * q1[1], q1[2] * q1[2], q1[0] * q1[1], q1[0], q1[1], q1[0] * 0.0, q1[0] * 0.0)
        v = jnp.concatenate(f, axis=0) * sums[48:56]
        extra = v if axis == 0 else extra + v
    sums = jnp.sum(fold8([*acc, psum, zero]) + extra, axis=1, keepdims=True)
    j0 = lax.broadcasted_iota(jnp.int32, (8, 128), 0)
    j1 = lax.broadcasted_iota(jnp.int32, (8, 128), 1)
    me = y * NROW + row
    bbox[me] = jnp.sum(jnp.where(j0 == j1, sums, 0.0), axis=0, keepdims=True)
    pl.semaphore_wait(sem_d, 3)
    for off in far_first():
        remote(bbox.at[me], bbox.at[me], b_r, at(*off)).start()

    newrow_ref[...] = jnp.sum(jnp.where(i0 == i1, state, 0.0), axis=0, keepdims=True)

    def updates(h):
        def piece(q, _):
            scales = lax.rsqrt(c[h, q])
            for j in range(PTILES):
                cols = pl.ds(pl.multiple_of(q * PCOLS + j * 128, 128), 128)
                for i in range(STEPS):
                    at_row = 8 * i + j if j < 8 else 24 + i
                    u[h, i, :, cols] = g[h, i, :, cols].astype(F32) * rr[i] * scales[at_row : at_row + 1]
            return 0

        return piece

    c_copy = remote(c.at[1], c.at[0], cp_r, pair)
    several(c.at[1], 6, c_r).wait_recv()
    c_copy.start()
    for h in (1, 0):
        if h == 0:
            c_copy.wait_recv()
        lax.fori_loop(0, PIECES, updates(h), 0)
        for q in range(PIECES):
            newcol_ref[h, q * PTILES : q * PTILES + 8, :] = c[h, q, 16:24, :]
            newcol_ref[h, q * PTILES + 8 : q * PTILES + 9, :] = c[h, q, 26:27, :]

    several(bbox, NALL - 1, b_r).wait_recv()
    sums = [bbox[i] for i in range(NALL)]
    while len(sums) > 1:
        sums = [sums[i] + sums[i + 1] for i in range(0, len(sums), 2)]
    sums = sums[0]
    j1 = lax.broadcasted_iota(jnp.int32, (1, 128), 1)
    uu0, uu1, uu2, u01, pu0, pu1, pp = [
        jnp.sum(jnp.where(j1 == m, sums, 0.0), axis=1, keepdims=True) for m in range(7)
    ]
    count = float(ROWS * COLS)
    clip = [jnp.minimum(1.0, lax.rsqrt(v * (1.0 / count))) for v in (uu0, uu1, uu2)]
    f0 = rate[0][2] * clip[0] * jnp.sqrt(pp * (1.0 / count))
    pp = pp - 2.0 * f0 * pu0 + f0 * f0 * uu0
    f1 = rate[1][2] * clip[1] * jnp.sqrt(pp * (1.0 / count))
    pp = pp - 2.0 * f1 * (pu1 - f0 * u01) + f1 * f1 * uu1
    f2 = rate[2][2] * clip[2] * jnp.sqrt(pp * (1.0 / count))
    for i, v in enumerate((f0, f1, f2)):
        factor_ref[i] = jnp.broadcast_to(v, (8, 128))

    remote(sent, sent, b_r, pair).wait_send()


def finish(p, u, factor_ref, newrow_ref, newcol_ref, out_hbm, row_hbm, col_hbm, o, written, out_sem, row_sem):
    k = lax.rem(lax.axis_index("row"), 2)
    halves = (1 - k, k)
    outs = [pltpu.make_async_copy(newrow_ref, row_hbm, row_sem)]
    for h in range(2):
        tiles = pl.ds(pl.multiple_of(halves[h] * HALF, 8), HALF)
        outs.append(pltpu.make_async_copy(newcol_ref.at[h], col_hbm.at[tiles], out_sem))
    for out in outs:
        out.start()
    f = [jnp.concatenate([factor_ref[i], factor_ref[i]], axis=0) for i in range(STEPS)]
    width = HCOLS // OUT_PARTS
    for h in range(2):
        for part in range(OUT_PARTS):
            for n in range(width // 128):
                cols = pl.ds(part * width + n * 128, 128)
                a = p[h, :, cols] - f[0] * u[h, 0, :, cols]
                o[h, :, cols] = a - (f[1] * u[h, 1, :, cols] + f[2] * u[h, 2, :, cols])
            src = o.at[h, :, pl.ds(part * width, width)]
            dst = out_hbm.at[:, pl.ds(pl.multiple_of(halves[h] * HCOLS + part * width, 128), width)]
            pltpu.make_async_copy(src, dst, out_sem).start()
    outs[0].wait()
    pltpu.make_async_copy(written, written, out_sem).wait()


def local(gradients, parameter, row_state, col_state):
    args = (gradients, parameter, row_state.reshape(1, LROWS), col_state.reshape(TILES, 128))
    vmem = pl.BlockSpec(memory_space=pltpu.VMEM)
    hbm = pl.BlockSpec(memory_space=pltpu.HBM)
    dma = pltpu.SemaphoreType.DMA
    regular, two = pltpu.SemaphoreType.REGULAR, dma((2,))
    state = pl.pallas_call(
        kernel,
        name="exchange",
        out_shape=(
            jax.ShapeDtypeStruct((2, LROWS, HCOLS), F32),
            jax.ShapeDtypeStruct((2, STEPS, LROWS, HCOLS), F32),
            jax.ShapeDtypeStruct((STEPS, 8, 128), F32),
            jax.ShapeDtypeStruct((1, LROWS), F32),
            jax.ShapeDtypeStruct((2, HALF, 128), F32),
        ),
        in_specs=[hbm] * 4,
        out_specs=(vmem,) * 5,
        scratch_shapes=[
            pltpu.VMEM((2, STEPS, LROWS, HCOLS), jnp.bfloat16),
            pltpu.VMEM((1, LROWS), F32),
            pltpu.VMEM((HALF, 128), F32),
            pltpu.VMEM((2, PIECES, SROWS, 128), F32),
            pltpu.VMEM((PIECES, SROWS, 128), F32),
            pltpu.VMEM((PIECES, SROWS, 128), F32),
            pltpu.VMEM((NX + NZ, SROWS, 128), F32),
            pltpu.VMEM((NZ + NX, SROWS, 128), F32),
            pltpu.VMEM((NY, 1, 128), F32),
            pltpu.VMEM((2, PIECES, WROWS, 128), F32),
            pltpu.VMEM((PIECES, WROWS, 128), F32),
            pltpu.VMEM((PIECES, WROWS, 128), F32),
            pltpu.VMEM((NX + NZ, WROWS, 128), F32),
            pltpu.VMEM((2, PIECES, SROWS, 128), F32),
            pltpu.VMEM((NALL, 1, 128), F32),
            pltpu.VMEM((LOADED, 1, 128), F32),
            pltpu.VMEM((SENT, 1, 128), F32),
            two, dma, dma, dma, two, two, dma, dma, two, two, dma, dma, dma, regular, regular, regular,
        ],
        compiler_params=pltpu.CompilerParams(
            collective_id=0, has_side_effects=True, vmem_limit_bytes=40 * 2**20
        ),
        cost_estimate=pl.CostEstimate(flops=20_000_000, bytes_accessed=4_200_000, transcendentals=100_000),
    )(*[pltpu.with_memory_space_constraint(a, pltpu.HBM) for a in args])
    new_param, new_row, new_col = pl.pallas_call(
        finish,
        name="finish",
        out_shape=(
            jax.ShapeDtypeStruct((LROWS, LCOLS), F32),
            jax.ShapeDtypeStruct((1, LROWS), F32),
            jax.ShapeDtypeStruct((TILES, 128), F32),
        ),
        in_specs=[vmem] * 5,
        out_specs=(hbm,) * 3,
        scratch_shapes=[
            pltpu.VMEM((2, LROWS, HCOLS), F32),
            pltpu.VMEM((LROWS * TILES + TILES, 1, 128), F32),
            dma, dma,
        ],
        compiler_params=pltpu.CompilerParams(vmem_limit_bytes=40 * 2**20),
        cost_estimate=pl.CostEstimate(flops=2_000_000, bytes_accessed=1_200_000, transcendentals=0),
    )(*state)
    return new_param, new_row.reshape(LROWS), new_col.reshape(LCOLS)


def solution(mesh):
    placed = (P(None, "row", "col"), P("row", "col"), P("row"), P("col"))
    return jax.shard_map(
        local,
        mesh=mesh,
        in_specs=placed,
        out_specs=(P("row", "col"), P("row"), P("col")),
        check_vma=False,
    )
```

```python
import functools

import jax
import jax.numpy as jnp
import numpy as np
from jax import lax
from jax.experimental import pallas as pl
from jax.experimental.pallas import tpu as pltpu
from jax.sharding import PartitionSpec as P

MESH = pl.DeviceIdType.MESH
START = 100
F32 = jnp.float32

NZ, NX, NK, NY = 4, 4, 2, 4
NROW, NALL = NZ * NX * NK, NZ * NX * NK * NY
STEPS, LROWS, LCOLS = 3, 16, 18432
ROWS, COLS = LROWS * NROW, LCOLS * NY
TILES = LCOLS // 128
HALF, HCOLS = TILES // 2, LCOLS // 2
PIECES = 8
PTILES = HALF // PIECES
PCOLS = PTILES * 128
SROWS = 32
WROWS = 56
PRODUCTS = 6
SENT = 2 * PIECES * SROWS + PIECES * WROWS + 6 * (3 * SROWS + WROWS) + NY - 1 + NALL - 1
LOADED = LROWS * TILES + HALF
OUT_PARTS = 6


def far_first():
    dist = (0, 1, 2, 1)
    offs = [(dz, dx, dy, dk) for dz in range(NZ) for dx in range(NX) for dy in range(NY) for dk in range(NK)]
    offs = [o for o in offs if o != (0, 0, 0, 0)]
    return sorted(offs, key=lambda o: (-(dist[o[0]] + dist[o[1]] + dist[o[2]]), -o[3]))


def rates():
    out = []
    for k in range(STEPS):
        t = np.float32(START + 1 + k)
        forget = np.float32(1.0) - np.power(t, np.float32(-0.8))
        out.append((float(forget), float(np.float32(1.0) - forget), float(np.power(t, np.float32(-0.5)))))
    return out


def up(x, n):
    return pltpu.roll(x, 8 - n, 0)


def down(x, n):
    return pltpu.roll(x, n, 0)


def fold8(v):
    s = lax.broadcasted_iota(jnp.int32, (8, 128), 0)
    m4, m2, m1 = s < 4, lax.rem(s, 4) < 2, lax.rem(s, 2) < 1
    w = [jnp.where(m4, v[i], v[i + 4]) + up(jnp.where(m4, v[i + 4], v[i]), 4) for i in range(4)]
    x = [jnp.where(m2, w[i] + up(w[i], 2), w[i + 2] + down(w[i + 2], 2)) for i in range(2)]
    return jnp.where(m1, x[0] + up(x[0], 1), x[1] + down(x[1], 1))


def kernel(
    grad_hbm, param_hbm, row_hbm, col_hbm,
    p, u, factor_ref, newrow_ref, newcol_ref,
    g, row_ref, col_ref, s, s_in, s_sum, r1, r2, rowbox, w, w_in, w_sum, wr, c, bbox, loaded, sent,
    g_sem, row_sem, load_sem, send, sp_r, r1_r, r2_r, box_r, wp_r, wr_r, c_r, cp_r, b_r, sem_p, sem_c, sem_d,
):
    rate = rates()
    row, y = lax.axis_index("row"), lax.axis_index("col")
    z, x, k = lax.div(row, 8), lax.rem(lax.div(row, 2), 4), lax.rem(row, 2)
    zz = [z, *[lax.rem(z + d, NZ) for d in range(1, NZ)]]
    xx = [x, *[lax.rem(x + d, NX) for d in range(1, NX)]]
    yy = [y, *[lax.rem(y + d, NY) for d in range(1, NY)]]
    kk = [k, 1 - k]

    def at(dz=0, dx=0, dy=0, dk=0):
        return (zz[dz] * 8 + xx[dx] * 2 + kk[dk], yy[dy])

    order = (2, 1, 3)
    pair = at(dk=1)
    xs = [at(dx=d) for d in order]
    zs = [at(dz=d) for d in order]
    ys = [at(dy=d) for d in order]

    def signal(sem, devices):
        for d in devices:
            pl.semaphore_signal(sem, inc=1, device_id=d, device_id_type=MESH)

    def remote(src, dst, recv, device):
        return pltpu.make_async_remote_copy(src, dst, send, recv, device_id=device, device_id_type=MESH)

    def several(ref, count, recv):
        return remote(ref.at[pl.ds(0, count)], ref.at[pl.ds(0, count)], recv, pair)

    halves = (1 - k, k)

    def columns(h):
        return pl.ds(pl.multiple_of(halves[h] * HCOLS, 128), HCOLS)

    barrier = pltpu.get_barrier_semaphore()
    g_loads = [pltpu.make_async_copy(grad_hbm.at[:, :, columns(h)], g.at[h], g_sem.at[h]) for h in range(2)]
    p_loads = [pltpu.make_async_copy(param_hbm.at[:, columns(h)], p.at[h], load_sem) for h in range(2)]
    col_load = pltpu.make_async_copy(col_hbm.at[pl.ds(pl.multiple_of(k * HALF, 8), HALF)], col_ref, load_sem)
    row_load = pltpu.make_async_copy(row_hbm, row_ref, row_sem)
    g_loads[0].start()
    signal(barrier, [(d[0] - k, d[1]) for d in (*zs, *xs, *ys)])

    @pl.when(k == 0)
    def _():
        signal(barrier, [pair])

    for load in (g_loads[1], row_load, col_load, *p_loads):
        load.start()

    lane = lax.broadcasted_iota(jnp.int32, (LROWS, 128), 1)
    sublane = lax.broadcasted_iota(jnp.int32, (LROWS, 128), 0)
    zero = jnp.zeros((8, 128), F32)

    def tile(h, i, n):
        return g[h, i, :, n * 128 : (n + 1) * 128].astype(F32)

    rows = [[None] * 4 for _ in range(STEPS)]

    def squares(h):
        g_loads[h].wait()
        for q in range(PIECES):
            last = []
            for i in range(STEPS):
                sums = []
                for j in range(PTILES):
                    a = tile(h, i, q * PTILES + j)
                    a = a * a
                    rows[i][j % 4] = a if rows[i][j % 4] is None else rows[i][j % 4] + a
                    sums.append(a[:8] + a[8:])
                s[h, q, 8 * i : 8 * i + 8, :] = fold8(sums[:8])
                last.append(sums[8])
            s[h, q, 24:32, :] = fold8(last + [zero] * (8 - STEPS))

    sp_copies = [
        remote(s.at[0, pl.ds(m * 4, 4)], s_in.at[pl.ds(m * 4, 4)], sp_r.at[m], pair) for m in range(2)
    ]
    squares(0)

    @pl.when(k == 1)
    def _():
        pl.semaphore_wait(barrier, 1)
        signal(sem_p, [pair])

    @pl.when(k == 0)
    def _():
        pl.semaphore_wait(sem_p, 1)

    for copy in sp_copies:
        copy.start()
    squares(1)

    packed = jnp.zeros((LROWS, 128), F32)
    for i in range(STEPS):
        total = (rows[i][0] + rows[i][1]) + (rows[i][2] + rows[i][3])
        packed = jnp.where(lane == sublane + LROWS * i, jnp.sum(total, axis=1, keepdims=True), packed)
    rowbox[y] = jnp.sum(packed, axis=0, keepdims=True)

    @pl.when(k == 0)
    def _():
        pl.semaphore_wait(barrier, 18)
        signal(sem_p, [pair])

    @pl.when(k == 1)
    def _():
        pl.semaphore_wait(sem_p, 1)

    for d in ys:
        remote(rowbox.at[y], rowbox.at[y], box_r, d).start()

    def scatter_x(mine, ref, recv):
        ref[x] = mine[x]
        for n, d in enumerate(order):
            remote(mine.at[xx[d]], ref.at[x], recv, xs[n]).start()

    def scatter_z(mine, ref, recv):
        ref[4 + z] = mine[4 + z]
        for n, d in enumerate(order):
            remote(mine.at[4 + zz[d]], ref.at[4 + z], recv, zs[n]).start()

    def four(ref, first=0):
        return (ref[first] + ref[first + 1]) + (ref[first + 2] + ref[first + 3])

    sp_copies[0].wait_recv()
    for q in range(4):
        s_sum[q] = s[1, q] + s_in[q]
    scatter_x(s_sum, r1, r1_r.at[0])
    sp_copies[1].wait_recv()
    for q in range(4, 8):
        s_sum[q] = s[1, q] + s_in[q]
    scatter_z(s_sum, r1, r1_r.at[1])
    signal(sem_c, xs)

    def norm(h):
        def group(n, acc):
            for j in range(8):
                a = p[h, :, pl.ds(pl.multiple_of(n * 1024 + j * 128, 128), 128)]
                a = a * a
                acc = acc + (a[:8] + a[8:])
            return acc

        return group

    psum = zero
    pltpu.make_async_copy(loaded, loaded, load_sem).wait()
    for h in range(2):
        psum = lax.fori_loop(0, HCOLS // 1024, norm(h), psum)
    pl.semaphore_wait(sem_c, 3)
    signal(sem_d, zs)

    row_load.wait()
    i0 = lax.broadcasted_iota(jnp.int32, (LROWS, LROWS), 0)
    i1 = lax.broadcasted_iota(jnp.int32, (LROWS, LROWS), 1)
    state = jnp.sum(jnp.where(i0 == i1, row_ref[...], 0.0), axis=1, keepdims=True)
    several(rowbox, 3, box_r).wait_recv()
    totals = (rowbox[0] + rowbox[1]) + (rowbox[2] + rowbox[3])
    rr = []
    for i in range(STEPS):
        total = jnp.sum(jnp.where(lane == sublane + LROWS * i, totals, 0.0), axis=1, keepdims=True)
        state = rate[i][0] * state + rate[i][1] * (total / COLS)
        rr.append(jnp.broadcast_to(lax.rsqrt(state), (LROWS, 128)))

    def products(h):
        def piece(q, _):
            sums = [[] for _ in range(PRODUCTS)]
            for j in range(PTILES):
                cols = pl.ds(pl.multiple_of(q * PCOLS + j * 128, 128), 128)
                a = [g[h, i, :, cols].astype(F32) * rr[i] for i in range(STEPS)]
                b = p[h, :, cols]
                for m, v in enumerate((a[0] * a[0], a[1] * a[1], a[2] * a[2], a[0] * a[1], a[0] * b, a[1] * b)):
                    sums[m].append(v[:8] + v[8:])
            for m in range(PRODUCTS):
                w[h, q, 8 * m : 8 * m + 8, :] = fold8(sums[m][:8])
            w[h, q, 48:56, :] = fold8([*[v[8] for v in sums], zero, zero])
            if h == 0:
                remote(w.at[0, q], w_in.at[q], wp_r.at[lax.div(q, 4)], pair).start()
            return 0

        return piece

    wp_copies = [
        remote(w.at[0, pl.ds(m * 4, 4)], w_in.at[pl.ds(m * 4, 4)], wp_r.at[m], pair) for m in range(2)
    ]
    lax.fori_loop(0, PIECES, products(0), 0)

    several(r1, 3, r1_r.at[0]).wait_recv()
    r2[z] = four(r1)
    for d in zs:
        remote(r2.at[z], r2.at[z], r2_r, d).start()
    several(r1, 3, r1_r.at[1]).wait_recv()
    r2[4 + x] = four(r1, 4)
    for d in xs:
        remote(r2.at[4 + x], r2.at[4 + x], r2_r, d).start()

    lax.fori_loop(0, 4, products(1), 0)
    wp_copies[0].wait_recv()
    for q in range(4):
        w_sum[q] = w[1, q] + w_in[q]
    scatter_x(w_sum, wr, wr_r.at[0])
    lax.fori_loop(4, 8, products(1), 0)
    wp_copies[1].wait_recv()
    for q in range(4, 8):
        w_sum[q] = w[1, q] + w_in[q]
    scatter_z(w_sum, wr, wr_r.at[1])

    scale = []
    several(r2, 6, r2_r).wait_recv()
    for axis, mine in ((0, x), (1, z + 4)):
        sums = four(r2, 4 * axis)
        first = mine * PTILES
        state8, state1 = col_ref[pl.ds(first, 8), :], col_ref[pl.ds(first + 8, 1), :]
        scale8, scale1 = [], []
        for i in range(STEPS):
            state8 = rate[i][0] * state8 + rate[i][1] * (sums[8 * i : 8 * i + 8] / ROWS)
            state1 = rate[i][0] * state1 + rate[i][1] * (sums[24 + i : 25 + i] / ROWS)
            c[1, mine, 8 * i : 8 * i + 8, :] = state8
            c[1, mine, 24 + i : 25 + i, :] = state1
            scale8.append(lax.rsqrt(state8))
            scale1.append(lax.rsqrt(state1))
        scale.append((scale8, scale1))
        for d in zs if axis else xs:
            remote(c.at[1, mine], c.at[1, mine], c_r, d).start()

    acc = [None] * PRODUCTS
    extra = None
    for axis in range(2):
        several(wr, 3, wr_r.at[axis]).wait_recv()
        sums = four(wr, 4 * axis)
        q8, q1 = scale[axis]
        for m, f in enumerate((q8[0] * q8[0], q8[1] * q8[1], q8[2] * q8[2], q8[0] * q8[1], q8[0], q8[1])):
            v = f * sums[8 * m : 8 * m + 8]
            acc[m] = v if axis == 0 else acc[m] + v
        f = (q1[0] * q1[0], q1[1] * q1[1], q1[2] * q1[2], q1[0] * q1[1], q1[0], q1[1], q1[0] * 0.0, q1[0] * 0.0)
        v = jnp.concatenate(f, axis=0) * sums[48:56]
        extra = v if axis == 0 else extra + v
    sums = jnp.sum(fold8([*acc, psum, zero]) + extra, axis=1, keepdims=True)
    j0 = lax.broadcasted_iota(jnp.int32, (8, 128), 0)
    j1 = lax.broadcasted_iota(jnp.int32, (8, 128), 1)
    me = y * NROW + row
    bbox[me] = jnp.sum(jnp.where(j0 == j1, sums, 0.0), axis=0, keepdims=True)
    pl.semaphore_wait(sem_d, 3)
    for off in far_first():
        remote(bbox.at[me], bbox.at[me], b_r, at(*off)).start()

    newrow_ref[...] = jnp.sum(jnp.where(i0 == i1, state, 0.0), axis=0, keepdims=True)

    def updates(h):
        def piece(q, _):
            scales = lax.rsqrt(c[h, q])
            for j in range(PTILES):
                cols = pl.ds(pl.multiple_of(q * PCOLS + j * 128, 128), 128)
                for i in range(STEPS):
                    at_row = 8 * i + j if j < 8 else 24 + i
                    u[h, i, :, cols] = g[h, i, :, cols].astype(F32) * rr[i] * scales[at_row : at_row + 1]
            return 0

        return piece

    c_copy = remote(c.at[1], c.at[0], cp_r, pair)
    several(c.at[1], 6, c_r).wait_recv()
    c_copy.start()
    for h in (1, 0):
        if h == 0:
            c_copy.wait_recv()
        lax.fori_loop(0, PIECES, updates(h), 0)
        for q in range(PIECES):
            newcol_ref[h, q * PTILES : q * PTILES + 8, :] = c[h, q, 16:24, :]
            newcol_ref[h, q * PTILES + 8 : q * PTILES + 9, :] = c[h, q, 26:27, :]

    several(bbox, NALL - 1, b_r).wait_recv()
    sums = [bbox[i] for i in range(NALL)]
    while len(sums) > 1:
        sums = [sums[i] + sums[i + 1] for i in range(0, len(sums), 2)]
    sums = sums[0]
    j1 = lax.broadcasted_iota(jnp.int32, (1, 128), 1)
    uu0, uu1, uu2, u01, pu0, pu1, pp = [
        jnp.sum(jnp.where(j1 == m, sums, 0.0), axis=1, keepdims=True) for m in range(7)
    ]
    count = float(ROWS * COLS)
    clip = [jnp.minimum(1.0, lax.rsqrt(v * (1.0 / count))) for v in (uu0, uu1, uu2)]
    f0 = rate[0][2] * clip[0] * jnp.sqrt(pp * (1.0 / count))
    pp = pp - 2.0 * f0 * pu0 + f0 * f0 * uu0
    f1 = rate[1][2] * clip[1] * jnp.sqrt(pp * (1.0 / count))
    pp = pp - 2.0 * f1 * (pu1 - f0 * u01) + f1 * f1 * uu1
    f2 = rate[2][2] * clip[2] * jnp.sqrt(pp * (1.0 / count))
    for i, v in enumerate((f0, f1, f2)):
        factor_ref[i] = jnp.broadcast_to(v, (8, 128))

    remote(sent, sent, b_r, pair).wait_send()


def finish(p, u, factor_ref, newrow_ref, newcol_ref, out_hbm, row_hbm, col_hbm, o, written, out_sem, row_sem):
    k = lax.rem(lax.axis_index("row"), 2)
    halves = (1 - k, k)
    outs = [pltpu.make_async_copy(newrow_ref, row_hbm, row_sem)]
    for h in range(2):
        tiles = pl.ds(pl.multiple_of(halves[h] * HALF, 8), HALF)
        outs.append(pltpu.make_async_copy(newcol_ref.at[h], col_hbm.at[tiles], out_sem))
    for out in outs:
        out.start()
    f = [jnp.concatenate([factor_ref[i], factor_ref[i]], axis=0) for i in range(STEPS)]
    width = HCOLS // OUT_PARTS
    for h in range(2):
        for part in range(OUT_PARTS):
            for n in range(width // 128):
                cols = pl.ds(part * width + n * 128, 128)
                a = p[h, :, cols] - f[0] * u[h, 0, :, cols]
                o[h, :, cols] = a - (f[1] * u[h, 1, :, cols] + f[2] * u[h, 2, :, cols])
            src = o.at[h, :, pl.ds(part * width, width)]
            dst = out_hbm.at[:, pl.ds(pl.multiple_of(halves[h] * HCOLS + part * width, 128), width)]
            pltpu.make_async_copy(src, dst, out_sem).start(priority=part % 2)
    outs[0].wait()
    pltpu.make_async_copy(written, written, out_sem).wait()


def local(gradients, parameter, row_state, col_state):
    args = (gradients, parameter, row_state.reshape(1, LROWS), col_state.reshape(TILES, 128))
    vmem = pl.BlockSpec(memory_space=pltpu.VMEM)
    hbm = pl.BlockSpec(memory_space=pltpu.HBM)
    dma = pltpu.SemaphoreType.DMA
    regular, two = pltpu.SemaphoreType.REGULAR, dma((2,))
    state = pl.pallas_call(
        kernel,
        name="exchange",
        out_shape=(
            jax.ShapeDtypeStruct((2, LROWS, HCOLS), F32),
            jax.ShapeDtypeStruct((2, STEPS, LROWS, HCOLS), F32),
            jax.ShapeDtypeStruct((STEPS, 8, 128), F32),
            jax.ShapeDtypeStruct((1, LROWS), F32),
            jax.ShapeDtypeStruct((2, HALF, 128), F32),
        ),
        in_specs=[hbm] * 4,
        out_specs=(vmem,) * 5,
        scratch_shapes=[
            pltpu.VMEM((2, STEPS, LROWS, HCOLS), jnp.bfloat16),
            pltpu.VMEM((1, LROWS), F32),
            pltpu.VMEM((HALF, 128), F32),
            pltpu.VMEM((2, PIECES, SROWS, 128), F32),
            pltpu.VMEM((PIECES, SROWS, 128), F32),
            pltpu.VMEM((PIECES, SROWS, 128), F32),
            pltpu.VMEM((NX + NZ, SROWS, 128), F32),
            pltpu.VMEM((NZ + NX, SROWS, 128), F32),
            pltpu.VMEM((NY, 1, 128), F32),
            pltpu.VMEM((2, PIECES, WROWS, 128), F32),
            pltpu.VMEM((PIECES, WROWS, 128), F32),
            pltpu.VMEM((PIECES, WROWS, 128), F32),
            pltpu.VMEM((NX + NZ, WROWS, 128), F32),
            pltpu.VMEM((2, PIECES, SROWS, 128), F32),
            pltpu.VMEM((NALL, 1, 128), F32),
            pltpu.VMEM((LOADED, 1, 128), F32),
            pltpu.VMEM((SENT, 1, 128), F32),
            two, dma, dma, dma, two, two, dma, dma, two, two, dma, dma, dma, regular, regular, regular,
        ],
        compiler_params=pltpu.CompilerParams(
            collective_id=0, has_side_effects=True, vmem_limit_bytes=40 * 2**20
        ),
        cost_estimate=pl.CostEstimate(flops=20_000_000, bytes_accessed=4_200_000, transcendentals=100_000),
    )(*[pltpu.with_memory_space_constraint(a, pltpu.HBM) for a in args])
    new_param, new_row, new_col = pl.pallas_call(
        finish,
        name="finish",
        out_shape=(
            jax.ShapeDtypeStruct((LROWS, LCOLS), F32),
            jax.ShapeDtypeStruct((1, LROWS), F32),
            jax.ShapeDtypeStruct((TILES, 128), F32),
        ),
        in_specs=[vmem] * 5,
        out_specs=(hbm,) * 3,
        scratch_shapes=[
            pltpu.VMEM((2, LROWS, HCOLS), F32),
            pltpu.VMEM((LROWS * TILES + TILES, 1, 128), F32),
            dma, dma,
        ],
        compiler_params=pltpu.CompilerParams(vmem_limit_bytes=40 * 2**20),
        cost_estimate=pl.CostEstimate(flops=2_000_000, bytes_accessed=1_200_000, transcendentals=0),
    )(*state)
    return new_param, new_row.reshape(LROWS), new_col.reshape(LCOLS)


def solution(mesh):
    placed = (P(None, "row", "col"), P("row", "col"), P("row"), P("col"))
    return jax.shard_map(
        local,
        mesh=mesh,
        in_specs=placed,
        out_specs=(P("row", "col"), P("row"), P("col")),
        check_vma=False,
    )
```

```python
import functools

import jax
import jax.numpy as jnp
import numpy as np
from jax import lax
from jax.experimental import pallas as pl
from jax.experimental.pallas import tpu as pltpu
from jax.sharding import PartitionSpec as P

MESH = pl.DeviceIdType.MESH
START = 100
F32 = jnp.float32

NZ, NX, NK, NY = 4, 4, 2, 4
NROW, NALL = NZ * NX * NK, NZ * NX * NK * NY
STEPS, LROWS, LCOLS = 3, 16, 18432
ROWS, COLS = LROWS * NROW, LCOLS * NY
TILES = LCOLS // 128
HALF, HCOLS = TILES // 2, LCOLS // 2
PIECES = 8
PTILES = HALF // PIECES
PCOLS = PTILES * 128
SROWS = 32
WROWS = 56
PRODUCTS = 6
SENT = 2 * PIECES * SROWS + PIECES * WROWS + 6 * (3 * SROWS + WROWS) + NY - 1 + NALL - 1
LOADED = LROWS * TILES + HALF
OUT_PARTS = 6


def far_first():
    dist = (0, 1, 2, 1)
    offs = [(dz, dx, dy, dk) for dz in range(NZ) for dx in range(NX) for dy in range(NY) for dk in range(NK)]
    offs = [o for o in offs if o != (0, 0, 0, 0)]
    return sorted(offs, key=lambda o: (-(dist[o[0]] + dist[o[1]] + dist[o[2]]), -o[3]))


def rates():
    out = []
    for k in range(STEPS):
        t = np.float32(START + 1 + k)
        forget = np.float32(1.0) - np.power(t, np.float32(-0.8))
        out.append((float(forget), float(np.float32(1.0) - forget), float(np.power(t, np.float32(-0.5)))))
    return out


def up(x, n):
    return pltpu.roll(x, 8 - n, 0)


def down(x, n):
    return pltpu.roll(x, n, 0)


def fold8(v):
    s = lax.broadcasted_iota(jnp.int32, (8, 128), 0)
    m4, m2, m1 = s < 4, lax.rem(s, 4) < 2, lax.rem(s, 2) < 1
    w = [jnp.where(m4, v[i], v[i + 4]) + up(jnp.where(m4, v[i + 4], v[i]), 4) for i in range(4)]
    x = [jnp.where(m2, w[i] + up(w[i], 2), w[i + 2] + down(w[i + 2], 2)) for i in range(2)]
    return jnp.where(m1, x[0] + up(x[0], 1), x[1] + down(x[1], 1))


def kernel(
    grad_hbm, param_hbm, row_hbm, col_hbm,
    p, u, factor_ref, newrow_ref, newcol_ref,
    g, row_ref, col_ref, s, s_in, s_sum, r1, r2, rowbox, w, w_in, w_sum, wr, c, bbox, loaded, sent,
    g_sem, row_sem, load_sem, send, sp_r, r1_r, r2_r, box_r, wp_r, wr_r, c_r, cp_r, b_r, sem_p, sem_c, sem_d,
):
    rate = rates()
    row, y = lax.axis_index("row"), lax.axis_index("col")
    z, x, k = lax.div(row, 8), lax.rem(lax.div(row, 2), 4), lax.rem(row, 2)
    zz = [z, *[lax.rem(z + d, NZ) for d in range(1, NZ)]]
    xx = [x, *[lax.rem(x + d, NX) for d in range(1, NX)]]
    yy = [y, *[lax.rem(y + d, NY) for d in range(1, NY)]]
    kk = [k, 1 - k]

    def at(dz=0, dx=0, dy=0, dk=0):
        return (zz[dz] * 8 + xx[dx] * 2 + kk[dk], yy[dy])

    order = (2, 1, 3)
    pair = at(dk=1)
    xs = [at(dx=d) for d in order]
    zs = [at(dz=d) for d in order]
    ys = [at(dy=d) for d in order]

    def signal(sem, devices):
        for d in devices:
            pl.semaphore_signal(sem, inc=1, device_id=d, device_id_type=MESH)

    def remote(src, dst, recv, device):
        return pltpu.make_async_remote_copy(src, dst, send, recv, device_id=device, device_id_type=MESH)

    def several(ref, count, recv):
        return remote(ref.at[pl.ds(0, count)], ref.at[pl.ds(0, count)], recv, pair)

    halves = (1 - k, k)

    def columns(h):
        return pl.ds(pl.multiple_of(halves[h] * HCOLS, 128), HCOLS)

    barrier = pltpu.get_barrier_semaphore()
    g_loads = [pltpu.make_async_copy(grad_hbm.at[:, :, columns(h)], g.at[h], g_sem.at[h]) for h in range(2)]
    p_loads = [pltpu.make_async_copy(param_hbm.at[:, columns(h)], p.at[h], load_sem) for h in range(2)]
    col_load = pltpu.make_async_copy(col_hbm.at[pl.ds(pl.multiple_of(k * HALF, 8), HALF)], col_ref, load_sem)
    row_load = pltpu.make_async_copy(row_hbm, row_ref, row_sem)
    g_loads[0].start()
    signal(barrier, [(d[0] - k, d[1]) for d in (*zs, *xs, *ys)])

    @pl.when(k == 0)
    def _():
        signal(barrier, [pair])

    for load in (g_loads[1], row_load, col_load, *p_loads):
        load.start()

    lane = lax.broadcasted_iota(jnp.int32, (LROWS, 128), 1)
    sublane = lax.broadcasted_iota(jnp.int32, (LROWS, 128), 0)
    zero = jnp.zeros((8, 128), F32)

    def tile(h, i, n):
        return g[h, i, :, n * 128 : (n + 1) * 128].astype(F32)

    rows = [[None] * 4 for _ in range(STEPS)]

    def squares(h):
        g_loads[h].wait()
        for q in range(PIECES):
            last = []
            for i in range(STEPS):
                sums = []
                for j in range(PTILES):
                    a = tile(h, i, q * PTILES + j)
                    a = a * a
                    rows[i][j % 4] = a if rows[i][j % 4] is None else rows[i][j % 4] + a
                    sums.append(a[:8] + a[8:])
                s[h, q, 8 * i : 8 * i + 8, :] = fold8(sums[:8])
                last.append(sums[8])
            s[h, q, 24:32, :] = fold8(last + [zero] * (8 - STEPS))

    sp_copies = [
        remote(s.at[0, pl.ds(m * 4, 4)], s_in.at[pl.ds(m * 4, 4)], sp_r.at[m], pair) for m in range(2)
    ]
    squares(0)

    @pl.when(k == 1)
    def _():
        pl.semaphore_wait(barrier, 1)
        signal(sem_p, [pair])

    @pl.when(k == 0)
    def _():
        pl.semaphore_wait(sem_p, 1)

    for copy in sp_copies:
        copy.start()
    squares(1)

    packed = jnp.zeros((LROWS, 128), F32)
    for i in range(STEPS):
        total = (rows[i][0] + rows[i][1]) + (rows[i][2] + rows[i][3])
        packed = jnp.where(lane == sublane + LROWS * i, jnp.sum(total, axis=1, keepdims=True), packed)
    rowbox[y] = jnp.sum(packed, axis=0, keepdims=True)

    @pl.when(k == 0)
    def _():
        pl.semaphore_wait(barrier, 18)
        signal(sem_p, [pair])

    @pl.when(k == 1)
    def _():
        pl.semaphore_wait(sem_p, 1)

    for d in ys:
        remote(rowbox.at[y], rowbox.at[y], box_r, d).start()

    def scatter_x(mine, ref, recv):
        ref[x] = mine[x]
        for n, d in enumerate(order):
            remote(mine.at[xx[d]], ref.at[x], recv, xs[n]).start()

    def scatter_z(mine, ref, recv):
        ref[4 + z] = mine[4 + z]
        for n, d in enumerate(order):
            remote(mine.at[4 + zz[d]], ref.at[4 + z], recv, zs[n]).start()

    def four(ref, first=0):
        return (ref[first] + ref[first + 1]) + (ref[first + 2] + ref[first + 3])

    sp_copies[0].wait_recv()
    for q in range(4):
        s_sum[q] = s[1, q] + s_in[q]
    scatter_x(s_sum, r1, r1_r.at[0])
    sp_copies[1].wait_recv()
    for q in range(4, 8):
        s_sum[q] = s[1, q] + s_in[q]
    scatter_z(s_sum, r1, r1_r.at[1])
    signal(sem_c, xs)

    def norm(h):
        def group(n, acc):
            for j in range(8):
                a = p[h, :, pl.ds(pl.multiple_of(n * 1024 + j * 128, 128), 128)]
                a = a * a
                acc = acc + (a[:8] + a[8:])
            return acc

        return group

    psum = zero
    pltpu.make_async_copy(loaded, loaded, load_sem).wait()
    for h in range(2):
        psum = lax.fori_loop(0, HCOLS // 1024, norm(h), psum)
    pl.semaphore_wait(sem_c, 3)
    signal(sem_d, zs)

    row_load.wait()
    i0 = lax.broadcasted_iota(jnp.int32, (LROWS, LROWS), 0)
    i1 = lax.broadcasted_iota(jnp.int32, (LROWS, LROWS), 1)
    state = jnp.sum(jnp.where(i0 == i1, row_ref[...], 0.0), axis=1, keepdims=True)
    several(rowbox, 3, box_r).wait_recv()
    totals = (rowbox[0] + rowbox[1]) + (rowbox[2] + rowbox[3])
    rr = []
    for i in range(STEPS):
        total = jnp.sum(jnp.where(lane == sublane + LROWS * i, totals, 0.0), axis=1, keepdims=True)
        state = rate[i][0] * state + rate[i][1] * (total / COLS)
        rr.append(jnp.broadcast_to(lax.rsqrt(state), (LROWS, 128)))

    def products(h):
        def piece(q, _):
            sums = [[] for _ in range(PRODUCTS)]
            for j in range(PTILES):
                cols = pl.ds(pl.multiple_of(q * PCOLS + j * 128, 128), 128)
                a = [g[h, i, :, cols].astype(F32) * rr[i] for i in range(STEPS)]
                b = p[h, :, cols]
                for m, v in enumerate((a[0] * a[0], a[1] * a[1], a[2] * a[2], a[0] * a[1], a[0] * b, a[1] * b)):
                    sums[m].append(v[:8] + v[8:])
            for m in range(PRODUCTS):
                w[h, q, 8 * m : 8 * m + 8, :] = fold8(sums[m][:8])
            w[h, q, 48:56, :] = fold8([*[v[8] for v in sums], zero, zero])
            if h == 0:
                remote(w.at[0, q], w_in.at[q], wp_r.at[lax.div(q, 4)], pair).start()
            return 0

        return piece

    wp_copies = [
        remote(w.at[0, pl.ds(m * 4, 4)], w_in.at[pl.ds(m * 4, 4)], wp_r.at[m], pair) for m in range(2)
    ]
    lax.fori_loop(0, PIECES, products(0), 0)

    several(r1, 3, r1_r.at[0]).wait_recv()
    r2[z] = four(r1)
    for d in zs:
        remote(r2.at[z], r2.at[z], r2_r.at[0], d).start()
    several(r1, 3, r1_r.at[1]).wait_recv()
    r2[4 + x] = four(r1, 4)
    for d in xs:
        remote(r2.at[4 + x], r2.at[4 + x], r2_r.at[1], d).start()

    lax.fori_loop(0, 4, products(1), 0)
    wp_copies[0].wait_recv()
    for q in range(4):
        w_sum[q] = w[1, q] + w_in[q]
    scatter_x(w_sum, wr, wr_r.at[0])
    lax.fori_loop(4, 8, products(1), 0)
    wp_copies[1].wait_recv()
    for q in range(4, 8):
        w_sum[q] = w[1, q] + w_in[q]
    scatter_z(w_sum, wr, wr_r.at[1])

    scale = []
    for axis, mine in ((0, x), (1, z + 4)):
        several(r2, 3, r2_r.at[axis]).wait_recv()
        sums = four(r2, 4 * axis)
        first = mine * PTILES
        state8, state1 = col_ref[pl.ds(first, 8), :], col_ref[pl.ds(first + 8, 1), :]
        scale8, scale1 = [], []
        for i in range(STEPS):
            state8 = rate[i][0] * state8 + rate[i][1] * (sums[8 * i : 8 * i + 8] / ROWS)
            state1 = rate[i][0] * state1 + rate[i][1] * (sums[24 + i : 25 + i] / ROWS)
            c[1, mine, 8 * i : 8 * i + 8, :] = state8
            c[1, mine, 24 + i : 25 + i, :] = state1
            scale8.append(lax.rsqrt(state8))
            scale1.append(lax.rsqrt(state1))
        scale.append((scale8, scale1))
        for d in zs if axis else xs:
            remote(c.at[1, mine], c.at[1, mine], c_r, d).start()

    acc = [None] * PRODUCTS
    extra = None
    for axis in range(2):
        several(wr, 3, wr_r.at[axis]).wait_recv()
        sums = four(wr, 4 * axis)
        q8, q1 = scale[axis]
        for m, f in enumerate((q8[0] * q8[0], q8[1] * q8[1], q8[2] * q8[2], q8[0] * q8[1], q8[0], q8[1])):
            v = f * sums[8 * m : 8 * m + 8]
            acc[m] = v if axis == 0 else acc[m] + v
        f = (q1[0] * q1[0], q1[1] * q1[1], q1[2] * q1[2], q1[0] * q1[1], q1[0], q1[1], q1[0] * 0.0, q1[0] * 0.0)
        v = jnp.concatenate(f, axis=0) * sums[48:56]
        extra = v if axis == 0 else extra + v
    sums = jnp.sum(fold8([*acc, psum, zero]) + extra, axis=1, keepdims=True)
    j0 = lax.broadcasted_iota(jnp.int32, (8, 128), 0)
    j1 = lax.broadcasted_iota(jnp.int32, (8, 128), 1)
    me = y * NROW + row
    bbox[me] = jnp.sum(jnp.where(j0 == j1, sums, 0.0), axis=0, keepdims=True)
    pl.semaphore_wait(sem_d, 3)
    for off in far_first():
        remote(bbox.at[me], bbox.at[me], b_r, at(*off)).start()

    newrow_ref[...] = jnp.sum(jnp.where(i0 == i1, state, 0.0), axis=0, keepdims=True)

    def updates(h):
        def piece(q, _):
            scales = lax.rsqrt(c[h, q])
            for j in range(PTILES):
                cols = pl.ds(pl.multiple_of(q * PCOLS + j * 128, 128), 128)
                for i in range(STEPS):
                    at_row = 8 * i + j if j < 8 else 24 + i
                    u[h, i, :, cols] = g[h, i, :, cols].astype(F32) * rr[i] * scales[at_row : at_row + 1]
            return 0

        return piece

    c_copy = remote(c.at[1], c.at[0], cp_r, pair)
    several(c.at[1], 6, c_r).wait_recv()
    c_copy.start()
    for h in (1, 0):
        if h == 0:
            c_copy.wait_recv()
        lax.fori_loop(0, PIECES, updates(h), 0)
        for q in range(PIECES):
            newcol_ref[h, q * PTILES : q * PTILES + 8, :] = c[h, q, 16:24, :]
            newcol_ref[h, q * PTILES + 8 : q * PTILES + 9, :] = c[h, q, 26:27, :]

    several(bbox, NALL - 1, b_r).wait_recv()
    sums = [bbox[i] for i in range(NALL)]
    while len(sums) > 1:
        sums = [sums[i] + sums[i + 1] for i in range(0, len(sums), 2)]
    sums = sums[0]
    j1 = lax.broadcasted_iota(jnp.int32, (1, 128), 1)
    uu0, uu1, uu2, u01, pu0, pu1, pp = [
        jnp.sum(jnp.where(j1 == m, sums, 0.0), axis=1, keepdims=True) for m in range(7)
    ]
    count = float(ROWS * COLS)
    clip = [jnp.minimum(1.0, lax.rsqrt(v * (1.0 / count))) for v in (uu0, uu1, uu2)]
    f0 = rate[0][2] * clip[0] * jnp.sqrt(pp * (1.0 / count))
    pp = pp - 2.0 * f0 * pu0 + f0 * f0 * uu0
    f1 = rate[1][2] * clip[1] * jnp.sqrt(pp * (1.0 / count))
    pp = pp - 2.0 * f1 * (pu1 - f0 * u01) + f1 * f1 * uu1
    f2 = rate[2][2] * clip[2] * jnp.sqrt(pp * (1.0 / count))
    for i, v in enumerate((f0, f1, f2)):
        factor_ref[i] = jnp.broadcast_to(v, (8, 128))

    remote(sent, sent, b_r, pair).wait_send()


def finish(p, u, factor_ref, newrow_ref, newcol_ref, out_hbm, row_hbm, col_hbm, o, written, out_sem, row_sem):
    k = lax.rem(lax.axis_index("row"), 2)
    halves = (1 - k, k)
    outs = [pltpu.make_async_copy(newrow_ref, row_hbm, row_sem)]
    for h in range(2):
        tiles = pl.ds(pl.multiple_of(halves[h] * HALF, 8), HALF)
        outs.append(pltpu.make_async_copy(newcol_ref.at[h], col_hbm.at[tiles], out_sem))
    for out in outs:
        out.start()
    f = [jnp.concatenate([factor_ref[i], factor_ref[i]], axis=0) for i in range(STEPS)]
    width = HCOLS // OUT_PARTS
    for h in range(2):
        for part in range(OUT_PARTS):
            for n in range(width // 128):
                cols = pl.ds(part * width + n * 128, 128)
                a = p[h, :, cols] - f[0] * u[h, 0, :, cols]
                o[h, :, cols] = a - (f[1] * u[h, 1, :, cols] + f[2] * u[h, 2, :, cols])
            src = o.at[h, :, pl.ds(part * width, width)]
            dst = out_hbm.at[:, pl.ds(pl.multiple_of(halves[h] * HCOLS + part * width, 128), width)]
            pltpu.make_async_copy(src, dst, out_sem).start(priority=part % 2)
    outs[0].wait()
    pltpu.make_async_copy(written, written, out_sem).wait()


def local(gradients, parameter, row_state, col_state):
    args = (gradients, parameter, row_state.reshape(1, LROWS), col_state.reshape(TILES, 128))
    vmem = pl.BlockSpec(memory_space=pltpu.VMEM)
    hbm = pl.BlockSpec(memory_space=pltpu.HBM)
    dma = pltpu.SemaphoreType.DMA
    regular, two = pltpu.SemaphoreType.REGULAR, dma((2,))
    state = pl.pallas_call(
        kernel,
        name="exchange",
        out_shape=(
            jax.ShapeDtypeStruct((2, LROWS, HCOLS), F32),
            jax.ShapeDtypeStruct((2, STEPS, LROWS, HCOLS), F32),
            jax.ShapeDtypeStruct((STEPS, 8, 128), F32),
            jax.ShapeDtypeStruct((1, LROWS), F32),
            jax.ShapeDtypeStruct((2, HALF, 128), F32),
        ),
        in_specs=[hbm] * 4,
        out_specs=(vmem,) * 5,
        scratch_shapes=[
            pltpu.VMEM((2, STEPS, LROWS, HCOLS), jnp.bfloat16),
            pltpu.VMEM((1, LROWS), F32),
            pltpu.VMEM((HALF, 128), F32),
            pltpu.VMEM((2, PIECES, SROWS, 128), F32),
            pltpu.VMEM((PIECES, SROWS, 128), F32),
            pltpu.VMEM((PIECES, SROWS, 128), F32),
            pltpu.VMEM((NX + NZ, SROWS, 128), F32),
            pltpu.VMEM((NZ + NX, SROWS, 128), F32),
            pltpu.VMEM((NY, 1, 128), F32),
            pltpu.VMEM((2, PIECES, WROWS, 128), F32),
            pltpu.VMEM((PIECES, WROWS, 128), F32),
            pltpu.VMEM((PIECES, WROWS, 128), F32),
            pltpu.VMEM((NX + NZ, WROWS, 128), F32),
            pltpu.VMEM((2, PIECES, SROWS, 128), F32),
            pltpu.VMEM((NALL, 1, 128), F32),
            pltpu.VMEM((LOADED, 1, 128), F32),
            pltpu.VMEM((SENT, 1, 128), F32),
            two, dma, dma, dma, two, two, two, dma, two, two, dma, dma, dma, regular, regular, regular,
        ],
        compiler_params=pltpu.CompilerParams(
            collective_id=0, has_side_effects=True, vmem_limit_bytes=40 * 2**20
        ),
        cost_estimate=pl.CostEstimate(flops=20_000_000, bytes_accessed=4_200_000, transcendentals=100_000),
    )(*[pltpu.with_memory_space_constraint(a, pltpu.HBM) for a in args])
    new_param, new_row, new_col = pl.pallas_call(
        finish,
        name="finish",
        out_shape=(
            jax.ShapeDtypeStruct((LROWS, LCOLS), F32),
            jax.ShapeDtypeStruct((1, LROWS), F32),
            jax.ShapeDtypeStruct((TILES, 128), F32),
        ),
        in_specs=[vmem] * 5,
        out_specs=(hbm,) * 3,
        scratch_shapes=[
            pltpu.VMEM((2, LROWS, HCOLS), F32),
            pltpu.VMEM((LROWS * TILES + TILES, 1, 128), F32),
            dma, dma,
        ],
        compiler_params=pltpu.CompilerParams(vmem_limit_bytes=40 * 2**20),
        cost_estimate=pl.CostEstimate(flops=2_000_000, bytes_accessed=1_200_000, transcendentals=0),
    )(*state)
    return new_param, new_row.reshape(LROWS), new_col.reshape(LCOLS)


def solution(mesh):
    placed = (P(None, "row", "col"), P("row", "col"), P("row"), P("col"))
    return jax.shard_map(
        local,
        mesh=mesh,
        in_specs=placed,
        out_specs=(P("row", "col"), P("row"), P("col")),
        check_vma=False,
    )
```
